32 devices in a mesh: dp: 16 (over z, x, core), tensor: 2 (over y).
Axes of the slice: x: 2, y: 2, z: 4, core: 2. Of those that a mesh axis runs over, the one named last changes fastest.
Arguments:
- tokens: bfloat16 [512, 32, 1536], P('tensor', 'dp'), may hold values from -6 to 6
- cached_len: int32 [32], P('dp'), may hold values from 0 to 32768, as said below
- prompt_group: int32 [32], P('dp'), may hold values from 0 to 7, as said below
- attn_gain: float32 [1536], replicated, may hold values from 0.1 to 1.9
- w_query: bfloat16 [1536, 1536], P(None, 'tensor'), may hold values from -0.15625 to 0.15625
- key_matrix: bfloat16 [1536, 768], P(None, 'tensor'), may hold values from -0.15625 to 0.15625
- value_matrix: bfloat16 [1536, 768], P(None, 'tensor'), may hold values from -0.15625 to 0.15625
- w_out: bfloat16 [1536, 1536], P('tensor'), may hold values from -1.25 to 1.25
- window_cache_keys: bfloat16 [32, 4096, 768], P('dp', None, 'tensor'), may hold values from -400 to 400
- window_cache_values: bfloat16 [32, 4096, 768], P('dp', None, 'tensor'), may hold values from -6 to 6
- prompt_keys: bfloat16 [8, 4096, 768], P(None, 'dp', 'tensor'), may hold values from -6 to 6
- prompt_values: bfloat16 [8, 4096, 768], P(None, 'dp', 'tensor'), may hold values from -6 to 6
- mlp_gain: float32 [1536], replicated, may hold values from 0.1 to 1.9
- w_gate: bfloat16 [1536, 4096], P(None, 'tensor'), may hold values from -0.15625 to 0.15625
- w_up: bfloat16 [1536, 4096], P(None, 'tensor'), may hold values from -0.15625 to 0.15625
- w_down: bfloat16 [4096, 1536], P('tensor'), may hold values from -0.09375 to 0.09375
Outputs:
- output: bfloat16 [512, 32, 1536], P('tensor', 'dp')
The draws below stay inside these ranges and needn't reach their ends.
Inputs may be any that keep to these rules, and one draw needn't show every extreme that they name: `cached_len`: in each prompt group some request has no cached tokens, and exactly one request in all has 32768. `prompt_group`: every group holds 4 requests.
All inputs are finite; a program needn't handle non-finite values.
Results may differ from the reference program's by a relative error of at most 0.024.
Values may be sent and summed in bfloat16 or wider, within the bound.
No kernel may reach another device: no remote copies, remote signals or barrier semaphores. Data moves between devices by JAX's collectives and lax.ppermute only.
A program may use at most 192 MiB of HBM per device.

```python
import math
import jax
import jax.numpy as jnp
from jax import lax

MODEL_WIDTH = 1536
QUERY_HEADS = 16
KEY_VALUE_HEADS = 8
HEAD_SIZE = 96
FF = 4096
FRESH_TOKENS = 512
WINDOW_SPAN = 4096
SINKS = 4
PROMPT_TOKENS = 4096
PROMPT_GROUPS = 8
MAXLEN = 32768
REQUEST_TOTAL = 32
N_TENSOR = 2


def request_plan(key):
    order = jax.random.permutation(jax.random.fold_in(key, 11), REQUEST_TOTAL).astype(jnp.int32)
    groups = (order % PROMPT_GROUPS).astype(jnp.int32)
    exponent = jax.random.randint(jax.random.fold_in(key, 12), (REQUEST_TOTAL,), 0, 16, dtype=jnp.int32)
    mantissa = jax.random.randint(jax.random.fold_in(key, 13), (REQUEST_TOTAL,), 0, MAXLEN, dtype=jnp.int32)
    shifted = jnp.right_shift(mantissa, 15 - exponent)
    lengths = jnp.where(order < PROMPT_GROUPS, 0, jnp.where(order == PROMPT_GROUPS, MAXLEN, shifted)).astype(jnp.int32)
    return (groups, lengths)


def draw_cached_len(key, part):
    return request_plan(key)[1]


def draw_prompt_group(key, part):
    return request_plan(key)[0]


def draw_window_cache_keys(key, part):
    rotary_base = jax.random.normal(jax.random.fold_in(key, 21), (REQUEST_TOTAL, WINDOW_SPAN, KEY_VALUE_HEADS * HEAD_SIZE), jnp.float32)
    return jnp.clip(rotary_base, -6.0, 6.0).astype(jnp.bfloat16)


def block_levels(key, dims, cuts, least, largest):
    loudness, own = 1.0, jax.random.fold_in(key, 6)
    for axis_at, shards_of in cuts:
        draws = jnp.exp(jax.random.uniform(jax.random.fold_in(own, axis_at), (shards_of,), jnp.float32, least / len(cuts), largest / len(cuts)))
        loudness = loudness * jnp.repeat(draws, dims[axis_at] // shards_of).reshape([-1 if axis == axis_at else 1 for axis in range(len(dims))])
    return loudness


def centred(key, extent, deviation, reach, cuts=(), kind=jnp.bfloat16):
    level = block_levels(key, extent, cuts, -0.22, 0.18) if cuts else 1.0
    result = jax.random.normal(key, extent, jnp.float32) * deviation * level
    return jnp.minimum(jnp.maximum(result, -reach), reach).astype(kind)


def setup_inputs(seed: int = 0) -> dict:
    arg_keys = jax.random.split(jax.random.key(seed), 17)
    tokens = centred(arg_keys[0], (FRESH_TOKENS, REQUEST_TOTAL, MODEL_WIDTH), 1.0, 6.0, ((0, 2), (1, 16)))
    cached_len = draw_cached_len(jax.random.fold_in(arg_keys[16], 71), 0)
    prompt_group = draw_prompt_group(jax.random.fold_in(arg_keys[16], 71), 0)
    attn_gain = jnp.clip(1.0 + 0.18 * jax.random.normal(arg_keys[3], (MODEL_WIDTH,), jnp.float32), 0.1, 1.9)
    w_query = centred(arg_keys[4], (MODEL_WIDTH, QUERY_HEADS * HEAD_SIZE), MODEL_WIDTH ** -0.5, 0.15625, ((1, 2),))
    key_matrix = centred(arg_keys[5], (MODEL_WIDTH, KEY_VALUE_HEADS * HEAD_SIZE), MODEL_WIDTH ** -0.5, 0.15625, ((1, 2),))
    value_matrix = centred(arg_keys[6], (MODEL_WIDTH, KEY_VALUE_HEADS * HEAD_SIZE), MODEL_WIDTH ** -0.5, 0.15625, ((1, 2),))
    w_out = centred(arg_keys[7], (QUERY_HEADS * HEAD_SIZE, MODEL_WIDTH), (QUERY_HEADS * HEAD_SIZE // 64) ** -0.5, 1.25, ((0, 2),))
    window_cache_keys = draw_window_cache_keys(jax.random.fold_in(arg_keys[16], 71), 0)
    window_cache_values = centred(arg_keys[9], (REQUEST_TOTAL, WINDOW_SPAN, KEY_VALUE_HEADS * HEAD_SIZE), 1.0, 6.0, ((0, 16), (2, 2)))
    prompt_keys = centred(arg_keys[10], (PROMPT_GROUPS, PROMPT_TOKENS, KEY_VALUE_HEADS * HEAD_SIZE), 1.0, 6.0, ((1, 16), (2, 2)))
    prompt_values = centred(arg_keys[11], (PROMPT_GROUPS, PROMPT_TOKENS, KEY_VALUE_HEADS * HEAD_SIZE), 1.0, 6.0, ((1, 16), (2, 2)))
    mlp_gain = jnp.clip(1.0 + 0.18 * jax.random.normal(arg_keys[12], (MODEL_WIDTH,), jnp.float32), 0.1, 1.9)
    w_gate = centred(arg_keys[13], (MODEL_WIDTH, FF), MODEL_WIDTH ** -0.5, 0.15625, ((1, 2),))
    w_up = centred(arg_keys[14], (MODEL_WIDTH, FF), MODEL_WIDTH ** -0.5, 0.15625, ((1, 2),))
    w_down = centred(arg_keys[15], (FF, MODEL_WIDTH), FF ** -0.5, 0.09375, ((0, 2),))
    return {"tokens": tokens, "cached_len": cached_len, "prompt_group": prompt_group, "attn_gain": attn_gain, "w_query": w_query, "key_matrix": key_matrix, "value_matrix": value_matrix, "w_out": w_out, "window_cache_keys": window_cache_keys, "window_cache_values": window_cache_values, "prompt_keys": prompt_keys, "prompt_values": prompt_values, "mlp_gain": mlp_gain, "w_gate": w_gate, "w_up": w_up, "w_down": w_down}


rope_base = 10000.0
epsilon = 1e-05

def norm_rows(values, gain_vec):
    widened = values.astype(jnp.float32)
    factor = lax.rsqrt(lax.optimization_barrier(jnp.mean(widened * widened, axis=-1, keepdims=True)) + epsilon)
    return (widened * factor * gain_vec).astype(jnp.bfloat16)

def rotate(values, positions):
    half_dim = values.shape[-1] // 2
    frequency = rope_base ** (-2.0 * jnp.arange(half_dim, dtype=jnp.float32) / values.shape[-1])
    angles = positions.astype(jnp.float32)[..., None, None] * frequency
    cosine = jnp.cos(angles)
    sine_part = jnp.sin(angles)
    first_half = values[..., :half_dim]
    second_half = values[..., half_dim:]
    return jnp.concatenate([first_half * cosine - second_half * sine_part, second_half * cosine + first_half * sine_part], axis=-1)

def group_sum(left_side, right_side, pieces):
    column_count = left_side.shape[1] // pieces
    summed = jnp.zeros((left_side.shape[0], right_side.shape[1]), jnp.float32)
    for part_index in range(pieces):
        partial_value = jnp.dot(left_side[:, part_index * column_count:(part_index + 1) * column_count], right_side[part_index * column_count:(part_index + 1) * column_count], preferred_element_type=jnp.float32)
        partial_value = lax.optimization_barrier(partial_value.astype(jnp.bfloat16))
        summed = summed + partial_value.astype(jnp.float32)
    return summed

def reference(tokens, cached_len, prompt_group, attn_gain, w_query, key_matrix, value_matrix, w_out, window_cache_keys, window_cache_values, prompt_keys, prompt_values, mlp_gain, w_gate, w_up, w_down):
    query_group_width = QUERY_HEADS // KEY_VALUE_HEADS
    score_scale = 1.0 / math.sqrt(HEAD_SIZE)
    normed = norm_rows(tokens, attn_gain)
    flattened_rows = normed.reshape(FRESH_TOKENS * REQUEST_TOTAL, MODEL_WIDTH)
    queries = jnp.dot(flattened_rows, w_query, preferred_element_type=jnp.float32).reshape(FRESH_TOKENS, REQUEST_TOTAL, QUERY_HEADS, HEAD_SIZE)
    fresh_keys = jnp.dot(flattened_rows, key_matrix, preferred_element_type=jnp.float32).reshape(FRESH_TOKENS, REQUEST_TOTAL, KEY_VALUE_HEADS, HEAD_SIZE)
    fresh_values = jnp.dot(flattened_rows, value_matrix, preferred_element_type=jnp.float32).astype(jnp.bfloat16).reshape(FRESH_TOKENS, REQUEST_TOTAL, KEY_VALUE_HEADS, HEAD_SIZE)
    positions = PROMPT_TOKENS + cached_len[None, :] + jnp.arange(FRESH_TOKENS, dtype=jnp.int32)[:, None]
    queries = rotate(queries, positions).astype(jnp.bfloat16)
    fresh_keys = rotate(fresh_keys, positions).astype(jnp.bfloat16)

    def one_request(request_index):
        length = lax.dynamic_index_in_dim(cached_len, request_index, 0, keepdims=False)
        prompt_group_index = lax.dynamic_index_in_dim(prompt_group, request_index, 0, keepdims=False)
        request_query = lax.dynamic_index_in_dim(queries, request_index, 1, keepdims=False)
        own_key = lax.dynamic_index_in_dim(fresh_keys, request_index, 1, keepdims=False)
        own_value = lax.dynamic_index_in_dim(fresh_values, request_index, 1, keepdims=False)
        earlier_key = lax.dynamic_index_in_dim(window_cache_keys, request_index, 0, keepdims=False).reshape(WINDOW_SPAN, KEY_VALUE_HEADS, HEAD_SIZE)
        earlier_value = lax.dynamic_index_in_dim(window_cache_values, request_index, 0, keepdims=False).reshape(WINDOW_SPAN, KEY_VALUE_HEADS, HEAD_SIZE)
        common_prompt_key = lax.dynamic_index_in_dim(prompt_keys, prompt_group_index, 0, keepdims=False).reshape(PROMPT_TOKENS, KEY_VALUE_HEADS, HEAD_SIZE)
        common_prompt_value = lax.dynamic_index_in_dim(prompt_values, prompt_group_index, 0, keepdims=False).reshape(PROMPT_TOKENS, KEY_VALUE_HEADS, HEAD_SIZE)
        keys_all = jnp.concatenate([common_prompt_key, earlier_key, own_key], axis=0)
        values_all = jnp.concatenate([common_prompt_value, earlier_value, own_value], axis=0)
        row_ids = jnp.arange(FRESH_TOKENS, dtype=jnp.int32)[:, None]
        prefix_ids = jnp.arange(PROMPT_TOKENS, dtype=jnp.int32)[None, :]
        slot_ids = jnp.arange(WINDOW_SPAN, dtype=jnp.int32)[None, :]
        col_ids = jnp.arange(FRESH_TOKENS, dtype=jnp.int32)[None, :]
        horizon = PROMPT_TOKENS + length + row_ids - WINDOW_SPAN
        prefix_seen = (prefix_ids < SINKS) | (prefix_ids > horizon)
        window_seen = (slot_ids >= WINDOW_SPAN - length) & (slot_ids > row_ids)
        span_seen = col_ids <= row_ids
        visible = jnp.concatenate([prefix_seen, window_seen, span_seen], axis=1)
        grouped_queries = request_query.reshape(FRESH_TOKENS, KEY_VALUE_HEADS, query_group_width, HEAD_SIZE)

        def single_head(head_index):
            query_head = lax.dynamic_index_in_dim(grouped_queries, head_index, 1, keepdims=False).astype(jnp.float32)
            key_head = lax.dynamic_index_in_dim(keys_all, head_index, 1, keepdims=False).astype(jnp.float32)
            value_head = lax.dynamic_index_in_dim(values_all, head_index, 1, keepdims=False).astype(jnp.float32)
            scores = jnp.einsum('igd,kd->gik', query_head, key_head) * score_scale
            scores = jnp.where(visible[None], scores, -jnp.inf)
            row_peak = lax.optimization_barrier(jnp.max(scores, axis=-1, keepdims=True))
            weights = jnp.exp(scores - row_peak)
            summed = lax.optimization_barrier(jnp.sum(weights, axis=-1, keepdims=True))
            rounded = lax.optimization_barrier(weights.astype(jnp.bfloat16)).astype(jnp.float32)
            blended = jnp.einsum('gik,kd->gid', rounded, value_head) / summed
            return blended
        head_outputs = lax.map(single_head, jnp.arange(KEY_VALUE_HEADS, dtype=jnp.int32))
        return head_outputs.transpose(2, 0, 1, 3).reshape(FRESH_TOKENS, QUERY_HEADS * HEAD_SIZE).astype(jnp.bfloat16)
    attended = lax.map(one_request, jnp.arange(REQUEST_TOTAL, dtype=jnp.int32))
    attended = attended.transpose(1, 0, 2).reshape(FRESH_TOKENS * REQUEST_TOTAL, QUERY_HEADS * HEAD_SIZE)
    attn_part = group_sum(attended, w_out, N_TENSOR).reshape(FRESH_TOKENS, REQUEST_TOTAL, MODEL_WIDTH)
    residual = (tokens.astype(jnp.float32) + attn_part).astype(jnp.bfloat16)
    normed_mlp = norm_rows(residual, mlp_gain).reshape(FRESH_TOKENS * REQUEST_TOTAL, MODEL_WIDTH)
    gate_part = jnp.dot(normed_mlp, w_gate, preferred_element_type=jnp.float32)
    up_part = jnp.dot(normed_mlp, w_up, preferred_element_type=jnp.float32)
    hidden = (jax.nn.silu(gate_part) * up_part).astype(jnp.bfloat16)
    mlp_part = group_sum(hidden, w_down, N_TENSOR).reshape(FRESH_TOKENS, REQUEST_TOTAL, MODEL_WIDTH)
    return (residual.astype(jnp.float32) + mlp_part).astype(jnp.bfloat16)
```

```python
import functools
import math

import jax
import jax.numpy as jnp
from jax import lax
from jax.experimental import pallas as pl
from jax.experimental.pallas import tpu as pltpu
from jax.sharding import PartitionSpec as P

MODEL_WIDTH = 1536
HEAD_SIZE = 96
FRESH_TOKENS = 512
WINDOW_SPAN = 4096
SINKS = 4
PROMPT_TOKENS = 4096

rope_base = 10000.0
epsilon = 1e-05
far_below = -1e30
EXP2_SCALE = math.log2(math.e) / math.sqrt(HEAD_SIZE)
QUERY_TILE = 256
CACHE_BLOCK = 256
SUM_ROWS = 16


def norm_rows(values, gain_vec):
    widened = values.astype(jnp.float32)
    factor = lax.rsqrt(jnp.mean(widened * widened, axis=-1, keepdims=True) + epsilon)
    return (widened * factor * gain_vec).astype(jnp.bfloat16)


def rotate_columns(values, positions):
    requests, rows, tokens = values.shape
    half_dim = HEAD_SIZE // 2
    frequency = rope_base ** (-2.0 * jnp.arange(half_dim, dtype=jnp.float32) / HEAD_SIZE)
    angles = positions.astype(jnp.float32)[:, None, None, :] * frequency[None, None, :, None]
    cosine = jnp.cos(angles)
    sine_part = jnp.sin(angles)
    split = values.reshape(requests, rows // HEAD_SIZE, 2, half_dim, tokens)
    first_half = split[:, :, 0]
    second_half = split[:, :, 1]
    turned = jnp.concatenate(
        [
            first_half * cosine - second_half * sine_part,
            second_half * cosine + first_half * sine_part,
        ],
        axis=2,
    )
    return turned.astype(jnp.bfloat16).reshape(requests, rows, tokens)


def attention_kernel(
    group_ref,
    len_ref,
    q_ref,
    fresh_k_ref,
    fresh_v_ref,
    cache_k_ref,
    cache_v_ref,
    prompt_ref,
    out_ref,
    peak_ref,
    sum_ref,
):
    length = len_ref[pl.program_id(0)]
    heads = q_ref.shape[1] // HEAD_SIZE
    halves = FRESH_TOKENS // QUERY_TILE
    piece = prompt_ref.shape[3]
    pieces = prompt_ref.shape[0]
    peak_ref[...] = jnp.full(peak_ref.shape, far_below, jnp.float32)
    sum_ref[...] = jnp.zeros(sum_ref.shape, jnp.float32)

    def absorb(keys, values, visible, tiles=None):
        block = keys.shape[1]
        turned = keys.T
        widened = jnp.concatenate([values, jnp.ones((SUM_ROWS, block), jnp.bfloat16)], axis=0)
        for half in range(halves):
            if tiles is not None and half not in tiles:
                continue
            mask = None
            if visible is not None:
                key_ids = lax.broadcasted_iota(jnp.int32, (block, QUERY_TILE), 0)
                row_ids = lax.broadcasted_iota(jnp.int32, (block, QUERY_TILE), 1)
                mask = visible(key_ids, row_ids + half * QUERY_TILE)
            for head in range(heads):
                place = head * halves + half
                query = q_ref[
                    0,
                    head * HEAD_SIZE : (head + 1) * HEAD_SIZE,
                    half * QUERY_TILE : (half + 1) * QUERY_TILE,
                ]
                scores = jnp.dot(turned, query, preferred_element_type=jnp.float32)
                if mask is not None:
                    scores = jnp.where(mask, scores, far_below)
                old_peak = peak_ref[place : place + 1, :]
                new_peak = jnp.maximum(old_peak, jnp.max(scores, axis=0, keepdims=True))
                peak_ref[place : place + 1, :] = new_peak
                factor = jnp.exp2((old_peak - new_peak) * EXP2_SCALE)
                weights = jnp.exp2((scores - new_peak) * EXP2_SCALE).astype(jnp.bfloat16)
                sum_ref[place] = sum_ref[place] * factor + jnp.dot(
                    widened, weights, preferred_element_type=jnp.float32
                )

    for start in range(0, FRESH_TOKENS, QUERY_TILE):
        absorb(
            fresh_k_ref[0, :, start : start + QUERY_TILE],
            fresh_v_ref[0, :, start : start + QUERY_TILE],
            lambda keys, rows, start=start: keys + start <= rows,
            tiles=range(start // QUERY_TILE, halves),
        )

    def cache_step(masked, index):
        start = pl.multiple_of(index * CACHE_BLOCK, CACHE_BLOCK)
        columns = pl.ds(start, CACHE_BLOCK)
        absorb(
            cache_k_ref[0, :, columns],
            cache_v_ref[0, :, columns],
            (
                lambda keys, rows: (keys + start >= WINDOW_SPAN - length) & (keys + start > rows)
            )
            if masked
            else None,
        )

    cache_blocks = WINDOW_SPAN // CACHE_BLOCK
    first = jnp.maximum((WINDOW_SPAN - length) // CACHE_BLOCK, 0)
    clear = jnp.minimum(jnp.maximum(first + 1, FRESH_TOKENS // CACHE_BLOCK), cache_blocks)

    def prompt_step(masked, index):
        start = index * piece
        absorb(
            prompt_ref[index, 0, 0:HEAD_SIZE, :],
            prompt_ref[index, 0, HEAD_SIZE : 2 * HEAD_SIZE, :],
            (lambda keys, rows: (keys + start < SINKS) | (keys + start > length + rows))
            if masked
            else None,
        )

    def run(low, high, step):
        def body(index, carry):
            step(index)
            return carry

        lax.fori_loop(low, high, body, 0)

    run(first, clear, functools.partial(cache_step, True))
    run(clear, cache_blocks, functools.partial(cache_step, False))
    prompt_step(True, 0)
    begin = jnp.minimum(jnp.maximum((length + 1) // piece, 1), pieces)
    open_from = jnp.clip((length + FRESH_TOKENS - 1) // piece + 1, begin, pieces)
    run(begin, open_from, functools.partial(prompt_step, True))
    run(open_from, pieces, functools.partial(prompt_step, False))

    for head in range(heads):
        for half in range(halves):
            total = sum_ref[head * halves + half]
            out_ref[
                0,
                head * HEAD_SIZE : (head + 1) * HEAD_SIZE,
                half * QUERY_TILE : (half + 1) * QUERY_TILE,
            ] = (total[:HEAD_SIZE] / total[HEAD_SIZE : HEAD_SIZE + 1]).astype(jnp.bfloat16)


def attend(groups, lengths, queries, fresh_k, fresh_v, cache_k, cache_v, prompts, first_head):
    requests = queries.shape[0]
    group_width = queries.shape[1] // cache_k.shape[1]
    heads = prompts.shape[2] // (2 * HEAD_SIZE)
    pieces, piece = prompts.shape[0], prompts.shape[3]
    query_rows = group_width * HEAD_SIZE
    own = lambda r, h, *_: (r, first_head + h, 0)
    places = group_width * FRESH_TOKENS // QUERY_TILE
    scores = requests * heads * group_width * FRESH_TOKENS * (WINDOW_SPAN + FRESH_TOKENS)
    return pl.pallas_call(
        attention_kernel,
        grid_spec=pltpu.PrefetchScalarGridSpec(
            num_scalar_prefetch=2,
            grid=(requests, heads),
            in_specs=[
                pl.BlockSpec((1, query_rows, FRESH_TOKENS), own),
                pl.BlockSpec((1, HEAD_SIZE, FRESH_TOKENS), own),
                pl.BlockSpec((1, HEAD_SIZE, FRESH_TOKENS), own),
                pl.BlockSpec((1, HEAD_SIZE, WINDOW_SPAN), own),
                pl.BlockSpec((1, HEAD_SIZE, WINDOW_SPAN), own),
                pl.BlockSpec(
                    (pieces, 1, 2 * HEAD_SIZE, piece), lambda r, h, group, _: (0, group[r], h, 0)
                ),
            ],
            out_specs=pl.BlockSpec((1, query_rows, FRESH_TOKENS), lambda r, h, *_: (r, h, 0)),
            scratch_shapes=[
                pltpu.VMEM((max(places, 8), QUERY_TILE), jnp.float32),
                pltpu.VMEM((places, HEAD_SIZE + SUM_ROWS, QUERY_TILE), jnp.float32),
            ],
        ),
        out_shape=jax.ShapeDtypeStruct((requests, heads * query_rows, FRESH_TOKENS), jnp.bfloat16),
        compiler_params=pltpu.CompilerParams(
            dimension_semantics=("arbitrary", "arbitrary"), vmem_limit_bytes=40 * 1024 * 1024
        ),
        cost_estimate=pl.CostEstimate(
            flops=4 * 256 * scores,
            bytes_accessed=requests * heads * 4 * HEAD_SIZE * 2 * (WINDOW_SPAN + PROMPT_TOKENS),
            transcendentals=scores,
        ),
        name="attend",
    )(groups, lengths, queries, fresh_k, fresh_v, cache_k, cache_v, prompts)


def body(
    dp_size,
    tensor_size,
    tokens,
    cached_len,
    prompt_group,
    attn_gain,
    w_query,
    key_matrix,
    value_matrix,
    w_out,
    window_cache_keys,
    window_cache_values,
    prompt_keys,
    prompt_values,
    mlp_gain,
    w_gate,
    w_up,
    w_down,
):
    local_rows, local_reqs = tokens.shape[:2]
    query_cols = w_query.shape[1]
    key_cols = key_matrix.shape[1]
    key_heads = key_cols // HEAD_SIZE
    paired = tensor_size == 2 and dp_size % 2 == 0
    swap = [(0, 1), (1, 0)]
    across = [(rank, rank ^ 1) for rank in range(dp_size)]
    tensor_rank = lax.axis_index("tensor")
    core = lax.axis_index("dp") % 2

    chunk_heads = max(key_heads // 2, 1)
    chunks = key_heads // chunk_heads
    group_count, piece = prompt_keys.shape[:2]
    by_head = lambda a: a.transpose(0, 2, 1).reshape(group_count, key_heads, HEAD_SIZE, piece)
    packed = jnp.concatenate([by_head(prompt_keys), by_head(prompt_values)], axis=2)
    prompts = []
    for chunk in range(chunks):
        part = packed[:, chunk * chunk_heads : (chunk + 1) * chunk_heads].reshape(
            group_count, chunk_heads * 2 * HEAD_SIZE, piece
        )
        if prompts:
            part, prompts[-1] = lax.optimization_barrier((part, prompts[-1]))
        prompts.append(lax.all_gather(part, "dp", axis=0))

    source = norm_rows(tokens.transpose(1, 0, 2), attn_gain)
    if paired:
        other = lax.ppermute(source, "tensor", swap)
        low = tensor_rank == 0
        normed = jnp.concatenate(
            [jnp.where(low, source, other), jnp.where(low, other, source)], axis=1
        )
    else:
        normed = lax.all_gather(source, "tensor", axis=1, tiled=True)

    def fetch(weight, axis, after):
        if not paired:
            return [lax.all_gather(weight, "tensor", axis=axis, tiled=True)]
        weight, _ = lax.optimization_barrier((weight, after))
        half = weight.shape[axis] // 2
        sent = lax.dynamic_slice_in_dim(weight, core * half, half, axis)
        mine = lax.ppermute(sent, "tensor", swap)
        return [weight, mine, lax.ppermute(mine, "dp", across)]

    out_parts = fetch(w_out, 0, normed)
    gate_parts = fetch(w_gate, 1, out_parts[-1])
    up_parts = fetch(w_up, 1, gate_parts[-1])
    down_parts = fetch(w_down, 0, up_parts[-1])

    positions = (
        PROMPT_TOKENS + cached_len[:, None] + jnp.arange(FRESH_TOKENS, dtype=jnp.int32)[None, :]
    )

    def project(weight):
        return jnp.stack(
            [
                lax.dot_general(
                    weight,
                    normed[request],
                    (((0,), (1,)), ((), ())),
                    preferred_element_type=jnp.float32,
                )
                for request in range(local_reqs)
            ]
        )

    queries = rotate_columns(project(w_query), positions)
    fresh_keys = rotate_columns(project(key_matrix), positions)
    fresh_values = project(value_matrix).astype(jnp.bfloat16)
    past_keys = window_cache_keys.transpose(0, 2, 1)
    past_values = window_cache_values.transpose(0, 2, 1)

    chunk_cols = query_cols // chunks
    attn_part = jnp.zeros((local_reqs * local_rows, MODEL_WIDTH), jnp.float32)

    def add_out(total, attended, weight):
        return total + jnp.concatenate(
            [
                lax.dot_general(
                    attended[request],
                    weight,
                    (((0,), (0,)), ((), ())),
                    preferred_element_type=jnp.float32,
                )
                for request in range(local_reqs)
            ]
        )

    for chunk in range(chunks):
        attended = attend(
            prompt_group,
            cached_len,
            queries,
            fresh_keys,
            fresh_values,
            past_keys,
            past_values,
            prompts[chunk],
            chunk * chunk_heads,
        )
        if paired:
            mine = lax.dynamic_slice_in_dim(attended, tensor_rank * local_rows, local_rows, 2)
            sent = lax.dynamic_slice_in_dim(attended, (1 - tensor_rank) * local_rows, local_rows, 2)
            got = lax.ppermute(sent, "tensor", swap)
            own_rows = out_parts[0][chunk * chunk_cols : (chunk + 1) * chunk_cols]
            attn_part = add_out(attn_part, mine, own_rows)
            half = query_cols // 2
            other_rows = jnp.concatenate(
                [
                    jnp.where(core == 0, out_parts[1], out_parts[2]),
                    jnp.where(core == 0, out_parts[2], out_parts[1]),
                ]
            )[chunk * chunk_cols : (chunk + 1) * chunk_cols]
            attn_part = add_out(attn_part, got, other_rows)
        else:
            spread = lax.all_to_all(attended, "tensor", split_axis=2, concat_axis=1, tiled=True)
            rows = out_parts[0].reshape(tensor_size, chunks, chunk_cols, MODEL_WIDTH)[:, chunk]
            attn_part = add_out(
                attn_part, spread, rows.reshape(tensor_size * chunk_cols, MODEL_WIDTH)
            )

    own_tokens = tokens.transpose(1, 0, 2).reshape(local_reqs * local_rows, MODEL_WIDTH)
    residual = (own_tokens.astype(jnp.float32) + attn_part).astype(jnp.bfloat16)
    normed_mlp = norm_rows(residual, mlp_gain)
    mlp_part = jnp.zeros((local_reqs * local_rows, MODEL_WIDTH), jnp.float32)
    for gate, up, down in zip(gate_parts, up_parts, down_parts, strict=True):
        gate_part = jnp.dot(normed_mlp, gate, preferred_element_type=jnp.float32)
        up_part = jnp.dot(normed_mlp, up, preferred_element_type=jnp.float32)
        hidden = (jax.nn.silu(gate_part) * up_part).astype(jnp.bfloat16)
        mlp_part = mlp_part + jnp.dot(hidden, down, preferred_element_type=jnp.float32)
    result = (residual.astype(jnp.float32) + mlp_part).astype(jnp.bfloat16)
    return result.reshape(local_reqs, local_rows, MODEL_WIDTH).transpose(1, 0, 2)


def solution(mesh):
    in_specs = (
        P("tensor", "dp", None),
        P("dp"),
        P("dp"),
        P(),
        P(None, "tensor"),
        P(None, "tensor"),
        P(None, "tensor"),
        P("tensor", None),
        P("dp", None, "tensor"),
        P("dp", None, "tensor"),
        P(None, "dp", "tensor"),
        P(None, "dp", "tensor"),
        P(),
        P(None, "tensor"),
        P(None, "tensor"),
        P("tensor", None),
    )
    out_specs = P("tensor", "dp", None)
    return jax.shard_map(
        functools.partial(body, mesh.shape["dp"], mesh.shape["tensor"]),
        mesh=mesh,
        in_specs=in_specs,
        out_specs=out_specs,
        check_vma=False,
    )
```

```python
import functools
import math

import jax
import jax.numpy as jnp
from jax import lax
from jax.experimental import pallas as pl
from jax.experimental.pallas import tpu as pltpu
from jax.sharding import PartitionSpec as P

MODEL_WIDTH = 1536
HEAD_SIZE = 96
FRESH_TOKENS = 512
WINDOW_SPAN = 4096
SINKS = 4
PROMPT_TOKENS = 4096

rope_base = 10000.0
epsilon = 1e-05
far_below = -1e30
EXP2_SCALE = math.log2(math.e) / math.sqrt(HEAD_SIZE)
QUERY_TILE = 256
CACHE_BLOCK = 256
SUM_ROWS = 16


def norm_rows(values, gain_vec):
    widened = values.astype(jnp.float32)
    factor = lax.rsqrt(jnp.mean(widened * widened, axis=-1, keepdims=True) + epsilon)
    return (widened * factor * gain_vec).astype(jnp.bfloat16)


def rotate_columns(values, positions):
    requests, rows, tokens = values.shape
    half_dim = HEAD_SIZE // 2
    frequency = rope_base ** (-2.0 * jnp.arange(half_dim, dtype=jnp.float32) / HEAD_SIZE)
    angles = positions.astype(jnp.float32)[:, None, None, :] * frequency[None, None, :, None]
    cosine = jnp.cos(angles)
    sine_part = jnp.sin(angles)
    split = values.reshape(requests, rows // HEAD_SIZE, 2, half_dim, tokens)
    first_half = split[:, :, 0]
    second_half = split[:, :, 1]
    turned = jnp.concatenate(
        [
            first_half * cosine - second_half * sine_part,
            second_half * cosine + first_half * sine_part,
        ],
        axis=2,
    )
    return turned.astype(jnp.bfloat16).reshape(requests, rows, tokens)


def attention_kernel(
    group_ref,
    len_ref,
    q_ref,
    fresh_k_ref,
    fresh_v_ref,
    cache_k_ref,
    cache_v_ref,
    prompt_ref,
    out_ref,
    wide_ref,
    sum_ref,
    even_ref,
    odd_ref,
):
    length = len_ref[pl.program_id(0)]
    heads = q_ref.shape[1] // HEAD_SIZE
    pieces, piece = prompt_ref.shape[0], prompt_ref.shape[3]
    width = heads * FRESH_TOKENS
    tiles = [slice(start, start + QUERY_TILE) for start in range(0, width, QUERY_TILE)]
    for head in range(heads):
        wide_ref[:, head * FRESH_TOKENS : (head + 1) * FRESH_TOKENS] = q_ref[
            0, head * HEAD_SIZE : (head + 1) * HEAD_SIZE, :
        ]
    sum_ref[...] = jnp.zeros(sum_ref.shape, jnp.float32)

    def load_fresh(index):
        columns = slice(index * QUERY_TILE, (index + 1) * QUERY_TILE)
        return fresh_k_ref[0, :, columns], fresh_v_ref[0, :, columns]

    def load_cache(index):
        columns = pl.ds(pl.multiple_of(index * CACHE_BLOCK, CACHE_BLOCK), CACHE_BLOCK)
        return cache_k_ref[0, :, columns], cache_v_ref[0, :, columns]

    def load_prompt(index):
        return (
            prompt_ref[index, 0, 0:HEAD_SIZE, :],
            prompt_ref[index, 0, HEAD_SIZE : 2 * HEAD_SIZE, :],
        )

    def widen(values):
        return jnp.concatenate(
            [values, jnp.ones((SUM_ROWS, values.shape[1]), jnp.bfloat16)], axis=0
        )

    def digest(widened, scores, old_peak, tile):
        new_peak = jnp.maximum(old_peak, jnp.max(scores, axis=0, keepdims=True))
        weights = jnp.exp2((scores - new_peak) * EXP2_SCALE).astype(jnp.bfloat16)
        factor = jnp.exp2((old_peak - new_peak) * EXP2_SCALE)
        sum_ref[:, tile] = sum_ref[:, tile] * factor + jnp.dot(
            widened, weights, preferred_element_type=jnp.float32
        )
        return new_peak

    def masked_step(peak, loaded, visible, least=0):
        keys, values = loaded
        turned = keys.T
        widened = widen(values)
        scores = []
        for tile in tiles:
            raw = jnp.dot(turned, wide_ref[:, tile], preferred_element_type=jnp.float32)
            key_ids = lax.broadcasted_iota(jnp.int32, raw.shape, 0)
            row_ids = lax.broadcasted_iota(jnp.int32, raw.shape, 1) + tile.start % FRESH_TOKENS
            scores.append(jnp.where(visible(key_ids, row_ids), raw, far_below))
        peaks = []
        for tile, score in zip(tiles, scores, strict=True):
            old = peak[:, tile]
            if tile.start % FRESH_TOKENS + QUERY_TILE <= least:
                peaks.append(old)
            else:
                peaks.append(digest(widened, score, old, tile))
        return jnp.concatenate(peaks, axis=1)

    def masked(low, high, load, visible, peak):
        return lax.fori_loop(
            low, high, lambda index, peak: masked_step(peak, load(index), visible(index)), peak
        )

    def score_into(loaded, held_ref):
        turned = loaded[0].T
        for tile in tiles:
            held_ref[0 : turned.shape[0], tile] = jnp.dot(
                turned, wide_ref[:, tile], preferred_element_type=jnp.float32
            )

    def digest_all(loaded, peak, held_ref):
        widened = widen(loaded[1])
        block = widened.shape[1]
        return jnp.concatenate(
            [digest(widened, held_ref[0:block, tile], peak[:, tile], tile) for tile in tiles],
            axis=1,
        )

    def unmasked(low, high, load, peak):
        last = high - 1
        count = jnp.maximum(high - low, 0)

        def pair(step, peak):
            at = low + 2 * step
            score_into(load(at + 1), odd_ref)
            peak = digest_all(load(at), peak, even_ref)
            score_into(load(jnp.minimum(at + 2, last)), even_ref)
            return digest_all(load(at + 1), peak, odd_ref)

        @pl.when(count > 0)
        def _():
            score_into(load(low), even_ref)

        peak = lax.fori_loop(0, count // 2, pair, peak)
        return lax.fori_loop(
            0, count % 2, lambda _, peak: digest_all(load(last), peak, even_ref), peak
        )

    peak = jnp.full((1, width), far_below, jnp.float32)
    for index in range(FRESH_TOKENS // QUERY_TILE):
        start = index * QUERY_TILE
        peak = masked_step(
            peak,
            load_fresh(index),
            lambda keys, rows, start=start: keys + start <= rows,
            least=start,
        )

    cache_blocks = WINDOW_SPAN // CACHE_BLOCK
    first = jnp.maximum((WINDOW_SPAN - length) // CACHE_BLOCK, 0)
    clear = jnp.minimum(jnp.maximum(first + 1, FRESH_TOKENS // CACHE_BLOCK), cache_blocks)

    def cache_visible(index):
        start = index * CACHE_BLOCK
        return lambda keys, rows: (keys + start >= WINDOW_SPAN - length) & (keys + start > rows)

    def prompt_visible(index):
        start = index * piece
        return lambda keys, rows: (keys + start < SINKS) | (keys + start > length + rows)

    peak = masked(first, clear, load_cache, cache_visible, peak)
    peak = unmasked(clear, cache_blocks, load_cache, peak)
    peak = masked_step(peak, load_prompt(0), prompt_visible(0))
    begin = jnp.minimum(jnp.maximum((length + 1) // piece, 1), pieces)
    open_from = jnp.clip((length + FRESH_TOKENS - 1) // piece + 1, begin, pieces)
    peak = masked(begin, open_from, load_prompt, prompt_visible, peak)
    peak = unmasked(open_from, pieces, load_prompt, peak)

    for head in range(heads):
        total = sum_ref[:, head * FRESH_TOKENS : (head + 1) * FRESH_TOKENS]
        out_ref[0, head * HEAD_SIZE : (head + 1) * HEAD_SIZE, :] = (
            total[:HEAD_SIZE] / total[HEAD_SIZE : HEAD_SIZE + 1]
        ).astype(jnp.bfloat16)


def attend(groups, lengths, queries, fresh_k, fresh_v, cache_k, cache_v, prompts, first_head):
    requests = queries.shape[0]
    group_width = queries.shape[1] // cache_k.shape[1]
    heads = prompts.shape[2] // (2 * HEAD_SIZE)
    pieces, piece = prompts.shape[0], prompts.shape[3]
    query_rows = group_width * HEAD_SIZE
    own = lambda r, h, *_: (r, first_head + h, 0)
    width = group_width * FRESH_TOKENS
    return pl.pallas_call(
        attention_kernel,
        grid_spec=pltpu.PrefetchScalarGridSpec(
            num_scalar_prefetch=2,
            grid=(requests, heads),
            in_specs=[
                pl.BlockSpec((1, query_rows, FRESH_TOKENS), own),
                pl.BlockSpec((1, HEAD_SIZE, FRESH_TOKENS), own),
                pl.BlockSpec((1, HEAD_SIZE, FRESH_TOKENS), own),
                pl.BlockSpec((1, HEAD_SIZE, WINDOW_SPAN), own),
                pl.BlockSpec((1, HEAD_SIZE, WINDOW_SPAN), own),
                pl.BlockSpec(
                    (pieces, 1, 2 * HEAD_SIZE, piece), lambda r, h, group, _: (0, group[r], h, 0)
                ),
            ],
            out_specs=pl.BlockSpec((1, query_rows, FRESH_TOKENS), lambda r, h, *_: (r, h, 0)),
            scratch_shapes=[
                pltpu.VMEM((HEAD_SIZE, width), jnp.bfloat16),
                pltpu.VMEM((HEAD_SIZE + SUM_ROWS, width), jnp.float32),
                pltpu.VMEM((CACHE_BLOCK, width), jnp.float32),
                pltpu.VMEM((CACHE_BLOCK, width), jnp.float32),
            ],
        ),
        out_shape=jax.ShapeDtypeStruct((requests, heads * query_rows, FRESH_TOKENS), jnp.bfloat16),
        compiler_params=pltpu.CompilerParams(
            dimension_semantics=("arbitrary", "arbitrary"), vmem_limit_bytes=40 * 1024 * 1024
        ),
        cost_estimate=pl.CostEstimate(flops=1, bytes_accessed=1, transcendentals=0),
        name="attend",
    )(groups, lengths, queries, fresh_k, fresh_v, cache_k, cache_v, prompts)


def body(
    dp_size,
    tensor_size,
    tokens,
    cached_len,
    prompt_group,
    attn_gain,
    w_query,
    key_matrix,
    value_matrix,
    w_out,
    window_cache_keys,
    window_cache_values,
    prompt_keys,
    prompt_values,
    mlp_gain,
    w_gate,
    w_up,
    w_down,
):
    local_rows, local_reqs = tokens.shape[:2]
    query_cols = w_query.shape[1]
    key_cols = key_matrix.shape[1]
    key_heads = key_cols // HEAD_SIZE
    paired = tensor_size == 2 and dp_size % 2 == 0
    swap = [(0, 1), (1, 0)]
    across = [(rank, rank ^ 1) for rank in range(dp_size)]
    tensor_rank = lax.axis_index("tensor")
    core = lax.axis_index("dp") % 2

    chunk_heads = max(key_heads // 2, 1)
    chunks = key_heads // chunk_heads
    group_count, piece = prompt_keys.shape[:2]
    by_head = lambda a: a.transpose(0, 2, 1).reshape(group_count, key_heads, HEAD_SIZE, piece)
    packed = jnp.concatenate([by_head(prompt_keys), by_head(prompt_values)], axis=2)
    parts = [
        packed[:, chunk * chunk_heads : (chunk + 1) * chunk_heads].reshape(
            group_count, chunk_heads * 2 * HEAD_SIZE, piece
        )
        for chunk in range(chunks)
    ]
    prompts = [lax.all_gather(parts[0], "dp", axis=0)]

    source = norm_rows(tokens.transpose(1, 0, 2), attn_gain)
    weights = [w_gate, w_out, w_up, w_down]
    weight_axes = [1, 0, 1, 0]
    if paired:
        other = lax.ppermute(source, "tensor", swap)
        sent = []
        for weight, axis in zip(weights, weight_axes, strict=True):
            half = weight.shape[axis] // 2
            sent.append(lax.dynamic_slice_in_dim(weight, core * half, half, axis))
        other, *sent = lax.optimization_barrier((other, *sent))
        fetched = [lax.ppermute(sent[0], "tensor", swap)]
        low = tensor_rank == 0
        normed = jnp.concatenate(
            [jnp.where(low, source, other), jnp.where(low, other, source)], axis=1
        )
    else:
        fetched = []
        normed = lax.all_gather(source, "tensor", axis=1, tiled=True)
        weights = [
            lax.all_gather(weight, "tensor", axis=axis, tiled=True)
            for weight, axis in zip(weights, weight_axes, strict=True)
        ]

    positions = (
        PROMPT_TOKENS + cached_len[:, None] + jnp.arange(FRESH_TOKENS, dtype=jnp.int32)[None, :]
    )

    def project(weight):
        return jnp.stack(
            [
                lax.dot_general(
                    weight,
                    normed[request],
                    (((0,), (1,)), ((), ())),
                    preferred_element_type=jnp.float32,
                )
                for request in range(local_reqs)
            ]
        )

    queries = rotate_columns(project(w_query), positions)
    fresh_keys = rotate_columns(project(key_matrix), positions)
    fresh_values = project(value_matrix).astype(jnp.bfloat16)
    past_keys = window_cache_keys.transpose(0, 2, 1)
    past_values = window_cache_values.transpose(0, 2, 1)

    held = (prompts[0], queries, fresh_keys, fresh_values, past_keys, past_values)
    if paired:
        parts[1:], held, fetched, sent[1:] = lax.optimization_barrier(
            (parts[1:], held, fetched, sent[1:])
        )
        fetched += [lax.ppermute(part, "tensor", swap) for part in sent[1:]]
    else:
        parts[1:], held = lax.optimization_barrier((parts[1:], held))
    prompts[0], queries, fresh_keys, fresh_values, past_keys, past_values = held
    prompts += [lax.all_gather(part, "dp", axis=0) for part in parts[1:]]

    chunk_cols = query_cols // chunks
    attn_part = jnp.zeros((local_reqs * local_rows, MODEL_WIDTH), jnp.float32)

    def add_out(total, attended, weight):
        return total + jnp.concatenate(
            [
                lax.dot_general(
                    attended[request],
                    weight,
                    (((0,), (0,)), ((), ())),
                    preferred_element_type=jnp.float32,
                )
                for request in range(local_reqs)
            ]
        )

    parts_of = lambda chunk: slice(chunk * chunk_cols, (chunk + 1) * chunk_cols)
    swapped = []
    for chunk in range(chunks):
        attended = attend(
            prompt_group,
            cached_len,
            queries,
            fresh_keys,
            fresh_values,
            past_keys,
            past_values,
            prompts[chunk],
            chunk * chunk_heads,
        )
        if paired:
            if chunk == chunks - 1:
                attended, swapped, fetched = lax.optimization_barrier((attended, swapped, fetched))
            sent = lax.dynamic_slice_in_dim(attended, (1 - tensor_rank) * local_rows, local_rows, 2)
            swapped.append(lax.ppermute(sent, "tensor", swap))
            mine = lax.dynamic_slice_in_dim(attended, tensor_rank * local_rows, local_rows, 2)
            attn_part = add_out(attn_part, mine, w_out[parts_of(chunk)])
        else:
            spread = lax.all_to_all(attended, "tensor", split_axis=2, concat_axis=1, tiled=True)
            rows = weights[1].reshape(tensor_size, chunks, chunk_cols, MODEL_WIDTH)[:, chunk]
            attn_part = add_out(
                attn_part, spread, rows.reshape(tensor_size * chunk_cols, MODEL_WIDTH)
            )
    hidden_sets = [(weights[0], *weights[2:])]
    if paired:
        passed = [lax.ppermute(part, "dp", across) for part in fetched]
        hidden_sets += [(fetched[0], *fetched[2:]), (passed[0], *passed[2:])]
        first_core = core == 0
        other_out = jnp.concatenate(
            [
                jnp.where(first_core, fetched[1], passed[1]),
                jnp.where(first_core, passed[1], fetched[1]),
            ]
        )
        for chunk in range(chunks):
            attn_part = add_out(attn_part, swapped[chunk], other_out[parts_of(chunk)])

    own_tokens = tokens.transpose(1, 0, 2).reshape(local_reqs * local_rows, MODEL_WIDTH)
    residual = (own_tokens.astype(jnp.float32) + attn_part).astype(jnp.bfloat16)
    normed_mlp = norm_rows(residual, mlp_gain)
    mlp_part = jnp.zeros((local_reqs * local_rows, MODEL_WIDTH), jnp.float32)
    for gate, up, down in hidden_sets:
        gate_part = jnp.dot(normed_mlp, gate, preferred_element_type=jnp.float32)
        up_part = jnp.dot(normed_mlp, up, preferred_element_type=jnp.float32)
        hidden = (jax.nn.silu(gate_part) * up_part).astype(jnp.bfloat16)
        mlp_part = mlp_part + jnp.dot(hidden, down, preferred_element_type=jnp.float32)
    result = (residual.astype(jnp.float32) + mlp_part).astype(jnp.bfloat16)
    return result.reshape(local_reqs, local_rows, MODEL_WIDTH).transpose(1, 0, 2)


def solution(mesh):
    in_specs = (
        P("tensor", "dp", None),
        P("dp"),
        P("dp"),
        P(),
        P(None, "tensor"),
        P(None, "tensor"),
        P(None, "tensor"),
        P("tensor", None),
        P("dp", None, "tensor"),
        P("dp", None, "tensor"),
        P(None, "dp", "tensor"),
        P(None, "dp", "tensor"),
        P(),
        P(None, "tensor"),
        P(None, "tensor"),
        P("tensor", None),
    )
    out_specs = P("tensor", "dp", None)
    return jax.shard_map(
        functools.partial(body, mesh.shape["dp"], mesh.shape["tensor"]),
        mesh=mesh,
        in_specs=in_specs,
        out_specs=out_specs,
        check_vma=False,
    )
```

```python
import functools
import math

import jax
import jax.numpy as jnp
from jax import lax
from jax.experimental import pallas as pl
from jax.experimental.pallas import tpu as pltpu
from jax.sharding import PartitionSpec as P

MODEL_WIDTH = 1536
HEAD_SIZE = 96
FRESH_TOKENS = 512
WINDOW_SPAN = 4096
SINKS = 4
PROMPT_TOKENS = 4096

rope_base = 10000.0
epsilon = 1e-05
far_below = -1e30
EXP2_SCALE = math.log2(math.e) / math.sqrt(HEAD_SIZE)
QUERY_TILE = 256
CACHE_BLOCK = 256
SUM_ROWS = 16
HIDDEN_TILE = 512


def norm_rows(values, gain_vec):
    widened = values.astype(jnp.float32)
    factor = lax.rsqrt(jnp.mean(widened * widened, axis=-1, keepdims=True) + epsilon)
    return (widened * factor * gain_vec).astype(jnp.bfloat16)


def rotate_columns(values, positions):
    requests, rows, tokens = values.shape
    half_dim = HEAD_SIZE // 2
    frequency = rope_base ** (-2.0 * jnp.arange(half_dim, dtype=jnp.float32) / HEAD_SIZE)
    angles = positions.astype(jnp.float32)[:, None, None, :] * frequency[None, None, :, None]
    cosine = jnp.cos(angles)
    sine_part = jnp.sin(angles)
    split = values.reshape(requests, rows // HEAD_SIZE, 2, half_dim, tokens)
    first_half = split[:, :, 0]
    second_half = split[:, :, 1]
    turned = jnp.concatenate(
        [
            first_half * cosine - second_half * sine_part,
            second_half * cosine + first_half * sine_part,
        ],
        axis=2,
    )
    return turned.astype(jnp.bfloat16).reshape(requests, rows, tokens)


def attention_kernel(
    group_ref,
    len_ref,
    q_ref,
    fresh_k_ref,
    fresh_v_ref,
    cache_k_ref,
    cache_v_ref,
    prompt_ref,
    out_ref,
    wide_ref,
    sum_ref,
    even_ref,
    odd_ref,
):
    length = len_ref[pl.program_id(0)]
    heads = q_ref.shape[1] // HEAD_SIZE
    pieces, piece = prompt_ref.shape[0], prompt_ref.shape[3]
    width = heads * FRESH_TOKENS
    tiles = [slice(start, start + QUERY_TILE) for start in range(0, width, QUERY_TILE)]
    for head in range(heads):
        wide_ref[:, head * FRESH_TOKENS : (head + 1) * FRESH_TOKENS] = q_ref[
            0, head * HEAD_SIZE : (head + 1) * HEAD_SIZE, :
        ]
    sum_ref[...] = jnp.zeros(sum_ref.shape, jnp.float32)

    def load_fresh(index):
        columns = slice(index * QUERY_TILE, (index + 1) * QUERY_TILE)
        return fresh_k_ref[0, :, columns], fresh_v_ref[0, :, columns]

    def load_cache(index):
        columns = pl.ds(pl.multiple_of(index * CACHE_BLOCK, CACHE_BLOCK), CACHE_BLOCK)
        return cache_k_ref[0, :, columns], cache_v_ref[0, :, columns]

    def load_prompt(index):
        return (
            prompt_ref[index, 0, 0:HEAD_SIZE, :],
            prompt_ref[index, 0, HEAD_SIZE : 2 * HEAD_SIZE, :],
        )

    def widen(values):
        return jnp.concatenate(
            [values, jnp.ones((SUM_ROWS, values.shape[1]), jnp.bfloat16)], axis=0
        )

    def digest(widened, scores, old_peak, tile):
        new_peak = jnp.maximum(old_peak, jnp.max(scores, axis=0, keepdims=True))
        weights = jnp.exp2((scores - new_peak) * EXP2_SCALE).astype(jnp.bfloat16)
        factor = jnp.exp2((old_peak - new_peak) * EXP2_SCALE)
        sum_ref[:, tile] = sum_ref[:, tile] * factor + jnp.dot(
            widened, weights, preferred_element_type=jnp.float32
        )
        return new_peak

    def masked_step(peak, loaded, visible, least=0):
        keys, values = loaded
        turned = keys.T
        widened = widen(values)
        scores = []
        for tile in tiles:
            raw = jnp.dot(turned, wide_ref[:, tile], preferred_element_type=jnp.float32)
            key_ids = lax.broadcasted_iota(jnp.int32, raw.shape, 0)
            row_ids = lax.broadcasted_iota(jnp.int32, raw.shape, 1) + tile.start % FRESH_TOKENS
            scores.append(jnp.where(visible(key_ids, row_ids), raw, far_below))
        peaks = []
        for tile, score in zip(tiles, scores, strict=True):
            old = peak[:, tile]
            if tile.start % FRESH_TOKENS + QUERY_TILE <= least:
                peaks.append(old)
            else:
                peaks.append(digest(widened, score, old, tile))
        return jnp.concatenate(peaks, axis=1)

    def masked(low, high, load, visible, peak):
        return lax.fori_loop(
            low, high, lambda index, peak: masked_step(peak, load(index), visible(index)), peak
        )

    def score_into(loaded, held_ref):
        turned = loaded[0].T
        for tile in tiles:
            held_ref[0 : turned.shape[0], tile] = jnp.dot(
                turned, wide_ref[:, tile], preferred_element_type=jnp.float32
            )

    def digest_all(loaded, peak, held_ref):
        widened = widen(loaded[1])
        block = widened.shape[1]
        return jnp.concatenate(
            [digest(widened, held_ref[0:block, tile], peak[:, tile], tile) for tile in tiles],
            axis=1,
        )

    def unmasked(low, high, load, peak):
        last = high - 1
        count = jnp.maximum(high - low, 0)

        def pair(step, peak):
            at = low + 2 * step
            score_into(load(at + 1), odd_ref)
            peak = digest_all(load(at), peak, even_ref)
            score_into(load(jnp.minimum(at + 2, last)), even_ref)
            return digest_all(load(at + 1), peak, odd_ref)

        @pl.when(count > 0)
        def _():
            score_into(load(low), even_ref)

        peak = lax.fori_loop(0, count // 2, pair, peak)
        return lax.fori_loop(
            0, count % 2, lambda _, peak: digest_all(load(last), peak, even_ref), peak
        )

    peak = jnp.full((1, width), far_below, jnp.float32)
    for index in range(FRESH_TOKENS // QUERY_TILE):
        start = index * QUERY_TILE
        peak = masked_step(
            peak,
            load_fresh(index),
            lambda keys, rows, start=start: keys + start <= rows,
            least=start,
        )

    cache_blocks = WINDOW_SPAN // CACHE_BLOCK
    first = jnp.maximum((WINDOW_SPAN - length) // CACHE_BLOCK, 0)
    clear = jnp.minimum(jnp.maximum(first + 1, FRESH_TOKENS // CACHE_BLOCK), cache_blocks)

    def cache_visible(index):
        start = index * CACHE_BLOCK
        return lambda keys, rows: (keys + start >= WINDOW_SPAN - length) & (keys + start > rows)

    def prompt_visible(index):
        start = index * piece
        return lambda keys, rows: (keys + start < SINKS) | (keys + start > length + rows)

    peak = masked(first, clear, load_cache, cache_visible, peak)
    peak = unmasked(clear, cache_blocks, load_cache, peak)
    peak = masked_step(peak, load_prompt(0), prompt_visible(0))
    begin = jnp.minimum(jnp.maximum((length + 1) // piece, 1), pieces)
    open_from = jnp.clip((length + FRESH_TOKENS - 1) // piece + 1, begin, pieces)
    peak = masked(begin, open_from, load_prompt, prompt_visible, peak)
    peak = unmasked(open_from, pieces, load_prompt, peak)

    for head in range(heads):
        total = sum_ref[:, head * FRESH_TOKENS : (head + 1) * FRESH_TOKENS]
        out_ref[0, head * HEAD_SIZE : (head + 1) * HEAD_SIZE, :] = (
            total[:HEAD_SIZE] / total[HEAD_SIZE : HEAD_SIZE + 1]
        ).astype(jnp.bfloat16)


def attend(groups, lengths, queries, fresh_k, fresh_v, cache_k, cache_v, prompts, first_head):
    requests = queries.shape[0]
    group_width = queries.shape[1] // cache_k.shape[1]
    heads = prompts.shape[2] // (2 * HEAD_SIZE)
    pieces, piece = prompts.shape[0], prompts.shape[3]
    query_rows = group_width * HEAD_SIZE
    own = lambda r, h, *_: (r, first_head + h, 0)
    width = group_width * FRESH_TOKENS
    return pl.pallas_call(
        attention_kernel,
        grid_spec=pltpu.PrefetchScalarGridSpec(
            num_scalar_prefetch=2,
            grid=(requests, heads),
            in_specs=[
                pl.BlockSpec((1, query_rows, FRESH_TOKENS), own),
                pl.BlockSpec((1, HEAD_SIZE, FRESH_TOKENS), own),
                pl.BlockSpec((1, HEAD_SIZE, FRESH_TOKENS), own),
                pl.BlockSpec((1, HEAD_SIZE, WINDOW_SPAN), own),
                pl.BlockSpec((1, HEAD_SIZE, WINDOW_SPAN), own),
                pl.BlockSpec(
                    (pieces, 1, 2 * HEAD_SIZE, piece), lambda r, h, group, _: (0, group[r], h, 0)
                ),
            ],
            out_specs=pl.BlockSpec((1, query_rows, FRESH_TOKENS), lambda r, h, *_: (r, h, 0)),
            scratch_shapes=[
                pltpu.VMEM((HEAD_SIZE, width), jnp.bfloat16),
                pltpu.VMEM((HEAD_SIZE + SUM_ROWS, width), jnp.float32),
                pltpu.VMEM((CACHE_BLOCK, width), jnp.float32),
                pltpu.VMEM((CACHE_BLOCK, width), jnp.float32),
            ],
        ),
        out_shape=jax.ShapeDtypeStruct((requests, heads * query_rows, FRESH_TOKENS), jnp.bfloat16),
        compiler_params=pltpu.CompilerParams(
            dimension_semantics=("arbitrary", "arbitrary"), vmem_limit_bytes=40 * 1024 * 1024
        ),
        cost_estimate=pl.CostEstimate(flops=1, bytes_accessed=1, transcendentals=0),
        name="attend",
    )(groups, lengths, queries, fresh_k, fresh_v, cache_k, cache_v, prompts)


def finish_kernel(counts, *refs):
    pair_count, set_count, tiles = counts
    heads = [refs[2 * pair : 2 * pair + 2] for pair in range(pair_count)]
    tokens_ref, gain_ref = refs[2 * pair_count : 2 * pair_count + 2]
    refs = refs[2 * pair_count + 2 :]
    sets = [refs[3 * index : 3 * index + 3] for index in range(set_count)]
    out_ref, normed_ref, total_ref = refs[3 * set_count :]
    step = pl.program_id(0)
    requests, rows = tokens_ref.shape[:2]

    @pl.when(step == 0)
    def _():
        for request in range(requests):
            summed = tokens_ref[request].astype(jnp.float32)
            for attended_ref, weight_ref in heads:
                summed = summed + jnp.dot(
                    attended_ref[request].T, weight_ref[...], preferred_element_type=jnp.float32
                )
            place = slice(request * rows, (request + 1) * rows)
            residual = summed.astype(jnp.bfloat16)
            normed_ref[place, :] = norm_rows(residual, gain_ref[...])
            total_ref[place, :] = residual.astype(jnp.float32)

    first = 0
    for (gate_ref, up_ref, down_ref), count in zip(sets, tiles, strict=True):

        @pl.when((step >= first) & (step < first + count))
        def _(gate_ref=gate_ref, up_ref=up_ref, down_ref=down_ref):
            normed = normed_ref[...]
            gate = jnp.dot(normed, gate_ref[...], preferred_element_type=jnp.float32)
            up = jnp.dot(normed, up_ref[...], preferred_element_type=jnp.float32)
            hidden = (gate / (1.0 + jnp.exp(-gate)) * up).astype(jnp.bfloat16)
            total_ref[...] += jnp.dot(hidden, down_ref[...], preferred_element_type=jnp.float32)

        first += count

    @pl.when(step == first - 1)
    def _():
        for request in range(requests):
            out_ref[request] = total_ref[request * rows : (request + 1) * rows, :].astype(
                jnp.bfloat16
            )


def finish(pairs, tokens, gain, sets):
    requests, rows, width = tokens.shape
    tile = min(HIDDEN_TILE, *(gate.shape[1] for gate, _, _ in sets))
    tiles = [gate.shape[1] // tile for gate, _, _ in sets]
    whole = lambda array: pl.BlockSpec(
        array.shape, lambda step: (0,) * array.ndim, pipeline_mode=pl.Buffered(1)
    )
    operands, specs = [], []
    for attended, weight in pairs:
        operands += [attended, weight]
        specs += [whole(attended), whole(weight)]
    gain = gain.reshape(1, width)
    operands += [tokens, gain]
    specs += [whole(tokens), whole(gain)]
    first = 0
    for (gate, up, down), count in zip(sets, tiles, strict=True):
        place = lambda step, first=first, count=count: jnp.clip(step - first, 0, count - 1)
        operands += [gate, up, down]
        specs += [
            pl.BlockSpec((width, tile), lambda step, place=place: (0, place(step))),
            pl.BlockSpec((width, tile), lambda step, place=place: (0, place(step))),
            pl.BlockSpec((tile, width), lambda step, place=place: (place(step), 0)),
        ]
        first += count
    return pl.pallas_call(
        functools.partial(finish_kernel, (len(pairs), len(sets), tiles)),
        grid=(first,),
        in_specs=specs,
        out_specs=pl.BlockSpec((requests, rows, width), lambda step: (0, 0, 0)),
        out_shape=jax.ShapeDtypeStruct((requests, rows, width), jnp.bfloat16),
        scratch_shapes=[
            pltpu.VMEM((requests * rows, width), jnp.bfloat16),
            pltpu.VMEM((requests * rows, width), jnp.float32),
        ],
        compiler_params=pltpu.CompilerParams(
            dimension_semantics=("arbitrary",), vmem_limit_bytes=56 * 1024 * 1024
        ),
        name="finish",
    )(*operands)


def body(
    dp_size,
    tensor_size,
    tokens,
    cached_len,
    prompt_group,
    attn_gain,
    w_query,
    key_matrix,
    value_matrix,
    w_out,
    window_cache_keys,
    window_cache_values,
    prompt_keys,
    prompt_values,
    mlp_gain,
    w_gate,
    w_up,
    w_down,
):
    local_rows, local_reqs = tokens.shape[:2]
    query_cols = w_query.shape[1]
    key_cols = key_matrix.shape[1]
    key_heads = key_cols // HEAD_SIZE
    paired = tensor_size == 2 and dp_size % 2 == 0 and key_heads % 2 == 0
    swap = [(0, 1), (1, 0)]
    across = [(rank, rank ^ 1) for rank in range(dp_size)]
    tensor_rank = lax.axis_index("tensor")
    core = lax.axis_index("dp") % 2

    chunk_heads = max(key_heads // 2, 1)
    chunks = key_heads // chunk_heads
    group_count, piece = prompt_keys.shape[:2]
    by_head = lambda a: a.transpose(0, 2, 1).reshape(group_count, key_heads, HEAD_SIZE, piece)
    packed = jnp.concatenate([by_head(prompt_keys), by_head(prompt_values)], axis=2)
    parts = [
        packed[:, chunk * chunk_heads : (chunk + 1) * chunk_heads].reshape(
            group_count, chunk_heads * 2 * HEAD_SIZE, piece
        )
        for chunk in range(chunks)
    ]
    prompts = [lax.all_gather(parts[0], "dp", axis=0)]

    source = norm_rows(tokens.transpose(1, 0, 2), attn_gain)
    weights = [w_gate, w_out, w_up, w_down]
    weight_axes = [1, 0, 1, 0]
    if paired:
        other = lax.ppermute(source, "tensor", swap)
        sent = []
        for weight, axis in zip(weights, weight_axes, strict=True):
            half = weight.shape[axis] // 2
            sent.append(lax.dynamic_slice_in_dim(weight, core * half, half, axis))
        other, *sent = lax.optimization_barrier((other, *sent))
        fetched = [lax.ppermute(sent[0], "tensor", swap)]
        low = tensor_rank == 0
        normed = jnp.concatenate(
            [jnp.where(low, source, other), jnp.where(low, other, source)], axis=1
        )
    else:
        fetched = []
        normed = lax.all_gather(source, "tensor", axis=1, tiled=True)
        weights = [
            lax.all_gather(weight, "tensor", axis=axis, tiled=True)
            for weight, axis in zip(weights, weight_axes, strict=True)
        ]

    positions = (
        PROMPT_TOKENS + cached_len[:, None] + jnp.arange(FRESH_TOKENS, dtype=jnp.int32)[None, :]
    )

    def project(weight):
        return jnp.stack(
            [
                lax.dot_general(
                    weight,
                    normed[request],
                    (((0,), (1,)), ((), ())),
                    preferred_element_type=jnp.float32,
                )
                for request in range(local_reqs)
            ]
        )

    queries = rotate_columns(project(w_query), positions)
    fresh_keys = rotate_columns(project(key_matrix), positions)
    fresh_values = project(value_matrix).astype(jnp.bfloat16)
    past_keys = window_cache_keys.transpose(0, 2, 1)
    past_values = window_cache_values.transpose(0, 2, 1)

    held = (prompts[0], queries, fresh_keys, fresh_values, past_keys, past_values)
    if paired:
        parts[1:], held, fetched, sent[1:] = lax.optimization_barrier(
            (parts[1:], held, fetched, sent[1:])
        )
        fetched += [lax.ppermute(part, "tensor", swap) for part in sent[1:]]
    else:
        parts[1:], held = lax.optimization_barrier((parts[1:], held))
    prompts[0], queries, fresh_keys, fresh_values, past_keys, past_values = held
    prompts += [lax.all_gather(part, "dp", axis=0) for part in parts[1:]]

    chunk_cols = query_cols // chunks
    pairs = []
    parts_of = lambda chunk: slice(chunk * chunk_cols, (chunk + 1) * chunk_cols)
    swapped = []
    for chunk in range(chunks):
        attended = attend(
            prompt_group,
            cached_len,
            queries,
            fresh_keys,
            fresh_values,
            past_keys,
            past_values,
            prompts[chunk],
            chunk * chunk_heads,
        )
        if paired:
            if chunk == chunks - 1:
                attended, swapped, fetched = lax.optimization_barrier((attended, swapped, fetched))
            sent = lax.dynamic_slice_in_dim(attended, (1 - tensor_rank) * local_rows, local_rows, 2)
            swapped.append(lax.ppermute(sent, "tensor", swap))
            mine = lax.dynamic_slice_in_dim(attended, tensor_rank * local_rows, local_rows, 2)
            pairs.append((mine, w_out[parts_of(chunk)]))
        else:
            spread = lax.all_to_all(attended, "tensor", split_axis=2, concat_axis=1, tiled=True)
            rows = weights[1].reshape(tensor_size, chunks, chunk_cols, MODEL_WIDTH)[:, chunk]
            pairs.append((spread, rows.reshape(tensor_size * chunk_cols, MODEL_WIDTH)))
    hidden_sets = [(weights[0], *weights[2:])]
    if paired:
        passed = [lax.ppermute(part, "dp", across) for part in fetched]
        hidden_sets += [(fetched[0], *fetched[2:]), (passed[0], *passed[2:])]
        first_core = core == 0
        pairs += [
            (jnp.where(first_core, swapped[0], swapped[1]), fetched[1]),
            (jnp.where(first_core, swapped[1], swapped[0]), passed[1]),
        ]
    result = finish(pairs, tokens.transpose(1, 0, 2), mlp_gain, hidden_sets)
    return result.transpose(1, 0, 2)


def solution(mesh):
    in_specs = (
        P("tensor", "dp", None),
        P("dp"),
        P("dp"),
        P(),
        P(None, "tensor"),
        P(None, "tensor"),
        P(None, "tensor"),
        P("tensor", None),
        P("dp", None, "tensor"),
        P("dp", None, "tensor"),
        P(None, "dp", "tensor"),
        P(None, "dp", "tensor"),
        P(),
        P(None, "tensor"),
        P(None, "tensor"),
        P("tensor", None),
    )
    out_specs = P("tensor", "dp", None)
    return jax.shard_map(
        functools.partial(body, mesh.shape["dp"], mesh.shape["tensor"]),
        mesh=mesh,
        in_specs=in_specs,
        out_specs=out_specs,
        check_vma=False,
    )
```

```python
import functools
import math

import jax
import jax.numpy as jnp
from jax import lax
from jax.experimental import pallas as pl
from jax.experimental.pallas import tpu as pltpu
from jax.sharding import PartitionSpec as P

MODEL_WIDTH = 1536
HEAD_SIZE = 96
FRESH_TOKENS = 512
WINDOW_SPAN = 4096
SINKS = 4
PROMPT_TOKENS = 4096

rope_base = 10000.0
epsilon = 1e-05
far_below = -1e30
EXP2_SCALE = math.log2(math.e) / math.sqrt(HEAD_SIZE)
QUERY_TILE = 256
CACHE_BLOCK = 256
SUM_ROWS = 16
SCORE_SCALE = 1.0 / math.sqrt(HEAD_SIZE)
HIDDEN_TILE = 512
LEVEL_TERMS = 3
LEVEL_ROWS = 16


def norm_rows(values, gain_vec):
    widened = values.astype(jnp.float32)
    factor = lax.rsqrt(jnp.mean(widened * widened, axis=-1, keepdims=True) + epsilon)
    return (widened * factor * gain_vec).astype(jnp.bfloat16)


def rotate_columns(values, positions):
    requests, rows, tokens = values.shape
    half_dim = HEAD_SIZE // 2
    frequency = rope_base ** (-2.0 * jnp.arange(half_dim, dtype=jnp.float32) / HEAD_SIZE)
    angles = positions.astype(jnp.float32)[:, None, None, :] * frequency[None, None, :, None]
    cosine = jnp.cos(angles)
    sine_part = jnp.sin(angles)
    split = values.reshape(requests, rows // HEAD_SIZE, 2, half_dim, tokens)
    first_half = split[:, :, 0]
    second_half = split[:, :, 1]
    turned = jnp.concatenate(
        [
            first_half * cosine - second_half * sine_part,
            second_half * cosine + first_half * sine_part,
        ],
        axis=2,
    )
    return turned.astype(jnp.bfloat16).reshape(requests, rows, tokens)


def attention_kernel(own, group_ref, len_ref, base_ref, q_ref, *refs):
    if own:
        fresh_k_ref, fresh_v_ref, cache_k_ref, cache_v_ref, *refs = refs
    prompt_ref, out_ref, wide_ref, sum_ref, even_ref, odd_ref = refs
    base = base_ref[0]
    length = len_ref[pl.program_id(0)]
    heads = q_ref.shape[1] // HEAD_SIZE
    pieces, piece = prompt_ref.shape[0], prompt_ref.shape[3]
    width = heads * FRESH_TOKENS
    tiles = [slice(start, start + QUERY_TILE) for start in range(0, width, QUERY_TILE)]
    for head in range(heads):
        wide_ref[:, head * FRESH_TOKENS : (head + 1) * FRESH_TOKENS] = q_ref[
            0, head * HEAD_SIZE : (head + 1) * HEAD_SIZE, :
        ]
    sum_ref[...] = jnp.zeros(sum_ref.shape, jnp.float32)

    def load_fresh(index):
        columns = slice(index * QUERY_TILE, (index + 1) * QUERY_TILE)
        return fresh_k_ref[0, :, columns], fresh_v_ref[0, :, columns]

    def load_cache(index):
        columns = pl.ds(pl.multiple_of(index * CACHE_BLOCK, CACHE_BLOCK), CACHE_BLOCK)
        return cache_k_ref[0, :, columns], cache_v_ref[0, :, columns]

    def load_prompt(index):
        return (
            prompt_ref[index, 0, 0:HEAD_SIZE, :],
            prompt_ref[index, 0, HEAD_SIZE : 2 * HEAD_SIZE, :],
        )

    def widen(values):
        return jnp.concatenate(
            [values, jnp.ones((SUM_ROWS, values.shape[1]), jnp.bfloat16)], axis=0
        )

    def digest(widened, scores, old_peak, tile):
        new_peak = jnp.maximum(old_peak, jnp.max(scores, axis=0, keepdims=True))
        weights = jnp.exp2((scores - new_peak) * EXP2_SCALE).astype(jnp.bfloat16)
        factor = jnp.exp2((old_peak - new_peak) * EXP2_SCALE)
        sum_ref[:, tile] = sum_ref[:, tile] * factor + jnp.dot(
            widened, weights, preferred_element_type=jnp.float32
        )
        return new_peak

    def masked_step(peak, loaded, visible, least=0):
        keys, values = loaded
        turned = keys.T
        widened = widen(values)
        scores = []
        for tile in tiles:
            raw = jnp.dot(turned, wide_ref[:, tile], preferred_element_type=jnp.float32)
            key_ids = lax.broadcasted_iota(jnp.int32, raw.shape, 0)
            row_ids = lax.broadcasted_iota(jnp.int32, raw.shape, 1) + tile.start % FRESH_TOKENS
            scores.append(jnp.where(visible(key_ids, row_ids), raw, far_below))
        peaks = []
        for tile, score in zip(tiles, scores, strict=True):
            old = peak[:, tile]
            if tile.start % FRESH_TOKENS + QUERY_TILE <= least:
                peaks.append(old)
            else:
                peaks.append(digest(widened, score, old, tile))
        return jnp.concatenate(peaks, axis=1)

    def masked(low, high, load, visible, peak):
        return lax.fori_loop(
            low, high, lambda index, peak: masked_step(peak, load(index), visible(index)), peak
        )

    def score_into(loaded, held_ref):
        turned = loaded[0].T
        for tile in tiles:
            held_ref[0 : turned.shape[0], tile] = jnp.dot(
                turned, wide_ref[:, tile], preferred_element_type=jnp.float32
            )

    def digest_all(loaded, peak, held_ref):
        widened = widen(loaded[1])
        block = widened.shape[1]
        return jnp.concatenate(
            [digest(widened, held_ref[0:block, tile], peak[:, tile], tile) for tile in tiles],
            axis=1,
        )

    def unmasked(low, high, load, peak):
        last = high - 1
        count = jnp.maximum(high - low, 0)

        def pair(step, peak):
            at = low + 2 * step
            score_into(load(at + 1), odd_ref)
            peak = digest_all(load(at), peak, even_ref)
            score_into(load(jnp.minimum(at + 2, last)), even_ref)
            return digest_all(load(at + 1), peak, odd_ref)

        @pl.when(count > 0)
        def _():
            score_into(load(low), even_ref)

        peak = lax.fori_loop(0, count // 2, pair, peak)
        return lax.fori_loop(
            0, count % 2, lambda _, peak: digest_all(load(last), peak, even_ref), peak
        )

    def cache_visible(index):
        start = index * CACHE_BLOCK
        return lambda keys, rows: (keys + start >= WINDOW_SPAN - length) & (keys + start > rows)

    def prompt_visible(index):
        start = base + index * piece
        return lambda keys, rows: (keys + start < SINKS) | (keys + start > length + rows)

    peak = jnp.full((1, width), far_below, jnp.float32)
    if own:
        for index in range(FRESH_TOKENS // QUERY_TILE):
            start = index * QUERY_TILE
            peak = masked_step(
                peak,
                load_fresh(index),
                lambda keys, rows, start=start: keys + start <= rows,
                least=start,
            )
        cache_blocks = WINDOW_SPAN // CACHE_BLOCK
        first = jnp.maximum((WINDOW_SPAN - length) // CACHE_BLOCK, 0)
        clear = jnp.minimum(jnp.maximum(first + 1, FRESH_TOKENS // CACHE_BLOCK), cache_blocks)
        peak = masked(first, clear, load_cache, cache_visible, peak)
        peak = unmasked(clear, cache_blocks, load_cache, peak)

    begin = jnp.clip((length + 1 - base) // piece, 0, pieces)
    open_from = jnp.clip((length + FRESH_TOKENS - 1 - base) // piece + 1, begin, pieces)
    sinks = jnp.where((base == 0) & (begin > 0), 1, 0)
    peak = masked(0, sinks, load_prompt, prompt_visible, peak)
    peak = masked(begin, open_from, load_prompt, prompt_visible, peak)
    peak = unmasked(open_from, pieces, load_prompt, peak)

    levels = []
    for head in range(heads):
        columns = slice(head * FRESH_TOKENS, (head + 1) * FRESH_TOKENS)
        total = sum_ref[:, columns]
        row_total = jnp.maximum(total[HEAD_SIZE : HEAD_SIZE + 1], 1e-30)
        out_ref[0, head * HEAD_SIZE : (head + 1) * HEAD_SIZE, :] = (
            total[:HEAD_SIZE] / row_total
        ).astype(jnp.bfloat16)
        rest = peak[:, columns] * SCORE_SCALE + jnp.log(row_total)
        for _ in range(LEVEL_TERMS):
            levels.append(rest.astype(jnp.bfloat16).astype(jnp.float32))
            rest = rest - levels[-1]
    levels.append(jnp.zeros((LEVEL_ROWS - len(levels), FRESH_TOKENS), jnp.float32))
    out_ref[0, heads * HEAD_SIZE :, :] = jnp.concatenate(levels, axis=0).astype(jnp.bfloat16)


def attend(groups, lengths, base, queries, own, prompts, first_head, group_width):
    requests = queries.shape[0]
    heads = prompts.shape[2] // (2 * HEAD_SIZE)
    pieces, piece = prompts.shape[0], prompts.shape[3]
    query_rows = group_width * HEAD_SIZE
    width = group_width * FRESH_TOKENS
    place = lambda r, h, *_: (r, first_head + h, 0)
    by_head = lambda r, h, *_: (r, h, 0)
    specs = [pl.BlockSpec((1, query_rows, FRESH_TOKENS), by_head)]
    if own:
        specs += [
            pl.BlockSpec((1, HEAD_SIZE, FRESH_TOKENS), place),
            pl.BlockSpec((1, HEAD_SIZE, FRESH_TOKENS), place),
            pl.BlockSpec((1, HEAD_SIZE, WINDOW_SPAN), place),
            pl.BlockSpec((1, HEAD_SIZE, WINDOW_SPAN), place),
        ]
    specs.append(
        pl.BlockSpec(
            (pieces, 1, 2 * HEAD_SIZE, piece), lambda r, h, group, *_: (0, group[r], h, 0)
        )
    )
    return pl.pallas_call(
        functools.partial(attention_kernel, bool(own)),
        grid_spec=pltpu.PrefetchScalarGridSpec(
            num_scalar_prefetch=3,
            grid=(requests, heads),
            in_specs=specs,
            out_specs=pl.BlockSpec((1, query_rows + LEVEL_ROWS, FRESH_TOKENS), by_head),
            scratch_shapes=[
                pltpu.VMEM((HEAD_SIZE, width), jnp.bfloat16),
                pltpu.VMEM((HEAD_SIZE + SUM_ROWS, width), jnp.float32),
                pltpu.VMEM((CACHE_BLOCK, width), jnp.float32),
                pltpu.VMEM((CACHE_BLOCK, width), jnp.float32),
            ],
        ),
        out_shape=jax.ShapeDtypeStruct(
            (requests, heads * (query_rows + LEVEL_ROWS), FRESH_TOKENS), jnp.bfloat16
        ),
        compiler_params=pltpu.CompilerParams(
            dimension_semantics=("arbitrary", "arbitrary"), vmem_limit_bytes=60 * 1024 * 1024
        ),
        cost_estimate=pl.CostEstimate(flops=1, bytes_accessed=1, transcendentals=0),
        name="attend",
    )(groups, lengths, base, queries, *own, prompts)


def merge(parts, heads, group_width):
    requests = parts[0].shape[0]
    query_rows = group_width * HEAD_SIZE
    outs, levels = [], []
    for part in parts:
        rows = part.reshape(requests, heads, query_rows + LEVEL_ROWS, FRESH_TOKENS)
        rows = rows.astype(jnp.float32)
        outs.append(
            rows[:, :, :query_rows].reshape(requests, heads, group_width, HEAD_SIZE, FRESH_TOKENS)
        )
        terms = rows[:, :, query_rows : query_rows + group_width * LEVEL_TERMS]
        levels.append(
            terms.reshape(requests, heads, group_width, LEVEL_TERMS, FRESH_TOKENS).sum(
                axis=3, keepdims=True
            )
        )
    top = functools.reduce(jnp.maximum, levels)
    shares = [jnp.exp(level - top) for level in levels]
    summed = sum(out * share for out, share in zip(outs, shares, strict=True))
    merged = (summed / sum(shares)).astype(jnp.bfloat16)
    return merged.reshape(requests, heads * query_rows, FRESH_TOKENS)


def finish_kernel(pair_count, plan, side_ref, *refs):
    heads = [refs[2 * pair : 2 * pair + 2] for pair in range(pair_count)]
    tokens_ref, gain_ref = refs[2 * pair_count : 2 * pair_count + 2]
    weights = refs[2 * pair_count + 2 : -7]
    out_ref, normed_ref, total_ref, gate_ref, up_ref, down_ref, arrived = refs[-7:]
    step = pl.program_id(0)
    requests, rows = tokens_ref.shape[:2]
    tile = gate_ref.shape[2]
    slots = gate_ref.shape[0]

    def copies(index):
        gate, gate_block, up, up_block, down, down_block = plan[index]
        slot = index % slots
        if gate_block == "side":
            gate_block = side_ref[0]
        elif gate_block == "far":
            gate_block = 1 - side_ref[0]
        gate_columns = pl.ds(pl.multiple_of(gate_block * tile, tile), tile)
        up_columns = pl.ds(up_block * tile, tile)
        down_rows = pl.ds(down_block * tile, tile)
        return [
            pltpu.make_async_copy(
                weights[gate].at[:, gate_columns], gate_ref.at[slot], arrived.at[slot, 0]
            ),
            pltpu.make_async_copy(
                weights[up].at[:, up_columns], up_ref.at[slot], arrived.at[slot, 1]
            ),
            pltpu.make_async_copy(
                weights[down].at[down_rows, :], down_ref.at[slot], arrived.at[slot, 2]
            ),
        ]

    @pl.when(step == 0)
    def _():
        for index in range(min(slots - 1, len(plan))):
            for copy in copies(index):
                copy.start()
        for request in range(requests):
            summed = tokens_ref[request].astype(jnp.float32)
            for attended_ref, weight_ref in heads:
                summed = summed + jnp.dot(
                    attended_ref[request].T, weight_ref[...], preferred_element_type=jnp.float32
                )
            place = slice(request * rows, (request + 1) * rows)
            residual = summed.astype(jnp.bfloat16)
            normed_ref[place, :] = norm_rows(residual, gain_ref[...])
            total_ref[place, :] = residual.astype(jnp.float32)

    for index in range(len(plan)):

        @pl.when(step == index)
        def _(index=index):
            if index + slots - 1 < len(plan):
                for copy in copies(index + slots - 1):
                    copy.start()
            for copy in copies(index):
                copy.wait()

    slot = step % slots
    normed = normed_ref[...]
    gate = jnp.dot(normed, gate_ref[slot], preferred_element_type=jnp.float32)
    up = jnp.dot(normed, up_ref[slot], preferred_element_type=jnp.float32)
    hidden = (gate / (1.0 + jnp.exp(-gate)) * up).astype(jnp.bfloat16)
    total_ref[...] += jnp.dot(hidden, down_ref[slot], preferred_element_type=jnp.float32)

    @pl.when(step == len(plan) - 1)
    def _():
        for request in range(requests):
            out_ref[request] = total_ref[request * rows : (request + 1) * rows, :].astype(
                jnp.bfloat16
            )


def finish(side, pairs, tokens, gain, weights, plan, tile):
    requests, rows, width = tokens.shape
    whole = lambda array: pl.BlockSpec(
        array.shape, lambda *_: (0,) * array.ndim, pipeline_mode=pl.Buffered(1)
    )
    operands, specs = [], []
    for attended, weight in pairs:
        operands += [attended, weight]
        specs += [whole(attended), whole(weight)]
    gain = gain.reshape(1, width)
    operands += [tokens, gain, *weights]
    specs += [whole(tokens), whole(gain)] + [pl.BlockSpec(memory_space=pl.ANY)] * len(weights)
    slots = 3
    return pl.pallas_call(
        functools.partial(finish_kernel, len(pairs), plan),
        grid_spec=pltpu.PrefetchScalarGridSpec(
            num_scalar_prefetch=1,
            grid=(len(plan),),
            in_specs=specs,
            out_specs=pl.BlockSpec((requests, rows, width), lambda *_: (0, 0, 0)),
            scratch_shapes=[
                pltpu.VMEM((requests * rows, width), jnp.bfloat16),
                pltpu.VMEM((requests * rows, width), jnp.float32),
                pltpu.VMEM((slots, width, tile), jnp.bfloat16),
                pltpu.VMEM((slots, width, tile), jnp.bfloat16),
                pltpu.VMEM((slots, tile, width), jnp.bfloat16),
                pltpu.SemaphoreType.DMA((slots, 3)),
            ],
        ),
        out_shape=jax.ShapeDtypeStruct((requests, rows, width), jnp.bfloat16),
        compiler_params=pltpu.CompilerParams(
            dimension_semantics=("arbitrary",), vmem_limit_bytes=56 * 1024 * 1024
        ),
        name="finish",
    )(side, *operands)


def body(
    dp_size,
    tensor_size,
    tokens,
    cached_len,
    prompt_group,
    attn_gain,
    w_query,
    key_matrix,
    value_matrix,
    w_out,
    window_cache_keys,
    window_cache_values,
    prompt_keys,
    prompt_values,
    mlp_gain,
    w_gate,
    w_up,
    w_down,
):
    local_rows, local_reqs = tokens.shape[:2]
    query_cols = w_query.shape[1]
    key_cols = key_matrix.shape[1]
    key_heads = key_cols // HEAD_SIZE
    hidden_cols = w_gate.shape[1]
    paired = tensor_size == 2 and dp_size % 4 == 0 and key_heads % 2 == 0
    swap = [(0, 1), (1, 0)]
    half_dp = dp_size // 2
    halves = [list(range(half_dp)), list(range(half_dp, dp_size))]
    to_core = [(rank, rank ^ 1) for rank in range(dp_size)]
    to_side = [(rank, rank ^ 2) for rank in range(dp_size)]
    to_half = [(rank, (rank + half_dp) % dp_size) for rank in range(dp_size)]
    tensor_rank = lax.axis_index("tensor")
    rank = lax.axis_index("dp")
    core, side = rank % 2, rank // 2 % 2

    own_tokens = tokens.transpose(1, 0, 2)
    source = norm_rows(own_tokens, attn_gain)

    chunk_heads = max(key_heads // 2, 1)
    chunks = key_heads // chunk_heads
    group_count, piece = prompt_keys.shape[:2]
    by_head = lambda a: a.transpose(0, 2, 1).reshape(group_count, key_heads, HEAD_SIZE, piece)
    packed = jnp.concatenate([by_head(prompt_keys), by_head(prompt_values)], axis=2)
    parts = [
        packed[:, chunk * chunk_heads : (chunk + 1) * chunk_heads].reshape(
            group_count, chunk_heads * 2 * HEAD_SIZE, piece
        )
        for chunk in range(chunks)
    ]
    gather = lambda part: lax.all_gather(part, "dp", axis=0, axis_index_groups=halves)
    prompts = [gather(parts[0])]
    base = (rank // half_dp * (half_dp * piece)).reshape(1)
    about = jnp.concatenate([cached_len, prompt_group])
    about_far = lax.ppermute(about, "dp", to_half)

    past = [window_cache_keys.transpose(0, 2, 1), window_cache_values.transpose(0, 2, 1)]
    sent = []
    if paired:
        other = lax.ppermute(source, "tensor", swap)
        for weight, axis, share in ((w_out, 0, 2), (w_up, 1, 4), (w_down, 0, 4), (w_gate, 1, 2)):
            count = weight.shape[axis] // 4
            start = core * 2 * count + (side * count if share == 4 else 0)
            sent.append(lax.dynamic_slice_in_dim(weight, start, weight.shape[axis] // share, axis))
        other, sent, past = lax.optimization_barrier((other, sent, past))
        out_mine = lax.ppermute(sent[0], "tensor", swap)
        low = tensor_rank == 0
        normed = jnp.concatenate(
            [jnp.where(low, source, other), jnp.where(low, other, source)], axis=1
        )
    else:
        normed = lax.all_gather(source, "tensor", axis=1, tiled=True)

    positions = (
        PROMPT_TOKENS + cached_len[:, None] + jnp.arange(FRESH_TOKENS, dtype=jnp.int32)[None, :]
    )

    def project(weight):
        return jnp.stack(
            [
                lax.dot_general(
                    weight,
                    normed[request],
                    (((0,), (1,)), ((), ())),
                    preferred_element_type=jnp.float32,
                )
                for request in range(local_reqs)
            ]
        )

    queries = rotate_columns(project(w_query), positions)
    chunk_cols = query_cols // chunks
    group_width = query_cols // key_cols
    parts_of = lambda chunk: slice(chunk * chunk_cols, (chunk + 1) * chunk_cols)
    asked = [queries[:, parts_of(chunk)] for chunk in range(chunks)]
    asked_far = [lax.ppermute(query, "dp", to_half) for query in asked]
    held = (prompts[0], asked, about_far)
    if paired:
        parts[1:], held, out_mine, sent[1:] = lax.optimization_barrier(
            (parts[1:], held, out_mine, sent[1:])
        )
        up_mine, down_mine = [lax.ppermute(part, "tensor", swap) for part in sent[1:3]]
    else:
        parts[1:], held = lax.optimization_barrier((parts[1:], held))
    prompts[0], asked, about_far = held
    prompts += [gather(part) for part in parts[1:]]

    own = [
        rotate_columns(project(key_matrix), positions),
        project(value_matrix).astype(jnp.bfloat16),
    ]
    asked_far[0], own, prompts[0], sent = lax.optimization_barrier(
        (asked_far[0], own, prompts[0], sent)
    )
    own += past
    if paired:
        gate_mine = lax.ppermute(sent[3], "tensor", swap)

    to_next = lambda part: lax.ppermute(part, "dp", to_side)
    hand = lambda part: lax.ppermute(part, "dp", to_core)
    far_lens, far_groups = about_far[:local_reqs], about_far[local_reqs:]
    attended, swapped = [], []
    for chunk in range(chunks):
        far = attend(
            far_groups, far_lens, base, asked_far[chunk], [], prompts[chunk], 0, group_width
        )
        far, asked[chunk] = lax.optimization_barrier((far, asked[chunk]))
        returned = lax.ppermute(far, "dp", to_half)
        if paired and chunk == 0:
            asked[chunk], up_mine = lax.optimization_barrier((asked[chunk], up_mine))
            up_side, up_core = to_next(up_mine), hand(up_mine)
        result = attend(
            prompt_group,
            cached_len,
            base,
            asked[chunk],
            own,
            prompts[chunk],
            chunk * chunk_heads,
            group_width,
        )
        if chunk < chunks - 1:
            result, asked_far[chunk + 1] = lax.optimization_barrier((result, asked_far[chunk + 1]))
            if paired:
                asked_far[chunk + 1], down_mine = lax.optimization_barrier(
                    (asked_far[chunk + 1], down_mine)
                )
                down_side, down_core = to_next(down_mine), hand(down_mine)
        else:
            result, returned = lax.optimization_barrier((result, returned))
        attended.append(merge([result, returned], chunk_heads, group_width))
        if paired:
            if chunk == chunks - 1:
                attended[-1], swapped, gate_mine, up_side, down_side = lax.optimization_barrier(
                    (attended[-1], swapped, gate_mine, up_side, down_side)
                )
            out_sent = lax.dynamic_slice_in_dim(
                attended[-1], (1 - tensor_rank) * local_rows, local_rows, 2
            )
            swapped.append(lax.ppermute(out_sent, "tensor", swap))

    pairs = []
    for chunk in range(chunks):
        if paired:
            mine = lax.dynamic_slice_in_dim(
                attended[chunk], tensor_rank * local_rows, local_rows, 2
            )
            pairs.append((mine, w_out[parts_of(chunk)]))
        else:
            spread = lax.all_to_all(
                attended[chunk], "tensor", split_axis=2, concat_axis=1, tiled=True
            )
            rows = lax.all_gather(w_out, "tensor", axis=0)
            rows = rows.reshape(tensor_size, chunks, chunk_cols, MODEL_WIDTH)[:, chunk]
            pairs.append((spread, rows.reshape(tensor_size * chunk_cols, MODEL_WIDTH)))
    if paired:
        tile = hidden_cols // 4
        weights = [w_gate, w_up, w_down, gate_mine, up_mine, down_mine, up_side, down_side]
        weights += [hand(gate_mine), up_core, down_core, hand(up_side), hand(down_side)]
        plan = [(0, block, 1, block, 2, block) for block in range(4)]
        plan += [(3, "side", 4, 0, 5, 0), (3, "far", 6, 0, 7, 0)]
        plan += [(8, "side", 9, 0, 10, 0), (8, "far", 11, 0, 12, 0)]
        first_core = core == 0
        pairs += [
            (jnp.where(first_core, swapped[0], swapped[1]), out_mine),
            (jnp.where(first_core, swapped[1], swapped[0]), hand(out_mine)),
        ]
    else:
        weights = [
            lax.all_gather(weight, "tensor", axis=axis, tiled=True)
            for weight, axis in ((w_gate, 1), (w_up, 1), (w_down, 0))
        ]
        tile = min(HIDDEN_TILE, hidden_cols)
        plan = [(0, block, 1, block, 2, block) for block in range(weights[0].shape[1] // tile)]
    result = finish(side.reshape(1), pairs, own_tokens, mlp_gain, weights, plan, tile)
    return result.transpose(1, 0, 2)


def solution(mesh):
    in_specs = (
        P("tensor", "dp", None),
        P("dp"),
        P("dp"),
        P(),
        P(None, "tensor"),
        P(None, "tensor"),
        P(None, "tensor"),
        P("tensor", None),
        P("dp", None, "tensor"),
        P("dp", None, "tensor"),
        P(None, "dp", "tensor"),
        P(None, "dp", "tensor"),
        P(),
        P(None, "tensor"),
        P(None, "tensor"),
        P("tensor", None),
    )
    out_specs = P("tensor", "dp", None)
    return jax.shard_map(
        functools.partial(body, mesh.shape["dp"], mesh.shape["tensor"]),
        mesh=mesh,
        in_specs=in_specs,
        out_specs=out_specs,
        check_vma=False,
    )
```

```python
import functools
import math

import jax
import jax.numpy as jnp
from jax import lax
from jax.experimental import pallas as pl
from jax.experimental.pallas import tpu as pltpu
from jax.sharding import PartitionSpec as P

MODEL_WIDTH = 1536
HEAD_SIZE = 96
FRESH_TOKENS = 512
WINDOW_SPAN = 4096
SINKS = 4
PROMPT_TOKENS = 4096

rope_base = 10000.0
epsilon = 1e-05
far_below = -1e30
EXP2_SCALE = math.log2(math.e) / math.sqrt(HEAD_SIZE)
QUERY_TILE = 256
CACHE_BLOCK = 256
SUM_ROWS = 16
SCORE_SCALE = 1.0 / math.sqrt(HEAD_SIZE)
HIDDEN_TILE = 512
LEVEL_TERMS = 3
LEVEL_ROWS = 16
LAST_FLOPS = 15 * 10**9


def norm_rows(values, gain_vec):
    widened = values.astype(jnp.float32)
    factor = lax.rsqrt(jnp.mean(widened * widened, axis=-1, keepdims=True) + epsilon)
    return (widened * factor * gain_vec).astype(jnp.bfloat16)


def rotate_columns(values, positions):
    requests, rows, tokens = values.shape
    half_dim = HEAD_SIZE // 2
    frequency = rope_base ** (-2.0 * jnp.arange(half_dim, dtype=jnp.float32) / HEAD_SIZE)
    angles = positions.astype(jnp.float32)[:, None, None, :] * frequency[None, None, :, None]
    cosine = jnp.cos(angles)
    sine_part = jnp.sin(angles)
    split = values.reshape(requests, rows // HEAD_SIZE, 2, half_dim, tokens)
    first_half = split[:, :, 0]
    second_half = split[:, :, 1]
    turned = jnp.concatenate(
        [
            first_half * cosine - second_half * sine_part,
            second_half * cosine + first_half * sine_part,
        ],
        axis=2,
    )
    return turned.astype(jnp.bfloat16).reshape(requests, rows, tokens)


def attention_kernel(own, group_ref, len_ref, base_ref, q_ref, *refs):
    if own:
        fresh_k_ref, fresh_v_ref, cache_k_ref, cache_v_ref, *refs = refs
    prompt_ref, out_ref, wide_ref, sum_ref, even_ref, odd_ref = refs
    base = base_ref[0]
    length = len_ref[pl.program_id(0)]
    heads = q_ref.shape[1] // HEAD_SIZE
    pieces, piece = prompt_ref.shape[0], prompt_ref.shape[3]
    width = heads * FRESH_TOKENS
    tiles = [slice(start, start + QUERY_TILE) for start in range(0, width, QUERY_TILE)]
    for head in range(heads):
        wide_ref[:, head * FRESH_TOKENS : (head + 1) * FRESH_TOKENS] = q_ref[
            0, head * HEAD_SIZE : (head + 1) * HEAD_SIZE, :
        ]
    sum_ref[...] = jnp.zeros(sum_ref.shape, jnp.float32)

    def load_fresh(index):
        columns = slice(index * QUERY_TILE, (index + 1) * QUERY_TILE)
        return fresh_k_ref[0, :, columns], fresh_v_ref[0, :, columns]

    def load_cache(index):
        columns = pl.ds(pl.multiple_of(index * CACHE_BLOCK, CACHE_BLOCK), CACHE_BLOCK)
        return cache_k_ref[0, :, columns], cache_v_ref[0, :, columns]

    def load_prompt(index):
        return (
            prompt_ref[index, 0, 0:HEAD_SIZE, :],
            prompt_ref[index, 0, HEAD_SIZE : 2 * HEAD_SIZE, :],
        )

    def widen(values):
        return jnp.concatenate(
            [values, jnp.ones((SUM_ROWS, values.shape[1]), jnp.bfloat16)], axis=0
        )

    def digest(widened, scores, old_peak, tile):
        new_peak = jnp.maximum(old_peak, jnp.max(scores, axis=0, keepdims=True))
        weights = jnp.exp2((scores - new_peak) * EXP2_SCALE).astype(jnp.bfloat16)
        factor = jnp.exp2((old_peak - new_peak) * EXP2_SCALE)
        sum_ref[:, tile] = sum_ref[:, tile] * factor + jnp.dot(
            widened, weights, preferred_element_type=jnp.float32
        )
        return new_peak

    def masked_step(peak, loaded, visible, least=0):
        keys, values = loaded
        turned = keys.T
        widened = widen(values)
        scores = []
        for tile in tiles:
            raw = jnp.dot(turned, wide_ref[:, tile], preferred_element_type=jnp.float32)
            key_ids = lax.broadcasted_iota(jnp.int32, raw.shape, 0)
            row_ids = lax.broadcasted_iota(jnp.int32, raw.shape, 1) + tile.start % FRESH_TOKENS
            scores.append(jnp.where(visible(key_ids, row_ids), raw, far_below))
        peaks = []
        for tile, score in zip(tiles, scores, strict=True):
            old = peak[:, tile]
            if tile.start % FRESH_TOKENS + QUERY_TILE <= least:
                peaks.append(old)
            else:
                peaks.append(digest(widened, score, old, tile))
        return jnp.concatenate(peaks, axis=1)

    def masked(low, high, load, visible, peak):
        return lax.fori_loop(
            low, high, lambda index, peak: masked_step(peak, load(index), visible(index)), peak
        )

    def score_into(loaded, held_ref):
        turned = loaded[0].T
        for tile in tiles:
            held_ref[0 : turned.shape[0], tile] = jnp.dot(
                turned, wide_ref[:, tile], preferred_element_type=jnp.float32
            )

    def digest_all(loaded, peak, held_ref):
        widened = widen(loaded[1])
        block = widened.shape[1]
        return jnp.concatenate(
            [digest(widened, held_ref[0:block, tile], peak[:, tile], tile) for tile in tiles],
            axis=1,
        )

    def unmasked(low, high, load, peak):
        last = high - 1
        count = jnp.maximum(high - low, 0)

        def pair(step, peak):
            at = low + 2 * step
            score_into(load(at + 1), odd_ref)
            peak = digest_all(load(at), peak, even_ref)
            score_into(load(jnp.minimum(at + 2, last)), even_ref)
            return digest_all(load(at + 1), peak, odd_ref)

        @pl.when(count > 0)
        def _():
            score_into(load(low), even_ref)

        peak = lax.fori_loop(0, count // 2, pair, peak)
        return lax.fori_loop(
            0, count % 2, lambda _, peak: digest_all(load(last), peak, even_ref), peak
        )

    def cache_visible(index):
        start = index * CACHE_BLOCK
        return lambda keys, rows: (keys + start >= WINDOW_SPAN - length) & (keys + start > rows)

    def prompt_visible(index):
        start = base + index * piece
        return lambda keys, rows: (keys + start < SINKS) | (keys + start > length + rows)

    peak = jnp.full((1, width), far_below, jnp.float32)
    if own:
        for index in range(FRESH_TOKENS // QUERY_TILE):
            start = index * QUERY_TILE
            peak = masked_step(
                peak,
                load_fresh(index),
                lambda keys, rows, start=start: keys + start <= rows,
                least=start,
            )
        cache_blocks = WINDOW_SPAN // CACHE_BLOCK
        first = jnp.maximum((WINDOW_SPAN - length) // CACHE_BLOCK, 0)
        clear = jnp.minimum(jnp.maximum(first + 1, FRESH_TOKENS // CACHE_BLOCK), cache_blocks)
        peak = masked(first, clear, load_cache, cache_visible, peak)
        peak = unmasked(clear, cache_blocks, load_cache, peak)

    begin = jnp.clip((length + 1 - base) // piece, 0, pieces)
    open_from = jnp.clip((length + FRESH_TOKENS - 1 - base) // piece + 1, begin, pieces)
    sinks = jnp.where((base == 0) & (begin > 0), 1, 0)
    peak = masked(0, sinks, load_prompt, prompt_visible, peak)
    peak = masked(begin, open_from, load_prompt, prompt_visible, peak)
    peak = unmasked(open_from, pieces, load_prompt, peak)

    levels = []
    for head in range(heads):
        columns = slice(head * FRESH_TOKENS, (head + 1) * FRESH_TOKENS)
        total = sum_ref[:, columns]
        row_total = jnp.maximum(total[HEAD_SIZE : HEAD_SIZE + 1], 1e-30)
        out_ref[0, head * HEAD_SIZE : (head + 1) * HEAD_SIZE, :] = (
            total[:HEAD_SIZE] / row_total
        ).astype(jnp.bfloat16)
        rest = peak[:, columns] * SCORE_SCALE + jnp.log(row_total)
        for _ in range(LEVEL_TERMS):
            levels.append(rest.astype(jnp.bfloat16).astype(jnp.float32))
            rest = rest - levels[-1]
    levels.append(jnp.zeros((LEVEL_ROWS - len(levels), FRESH_TOKENS), jnp.float32))
    out_ref[0, heads * HEAD_SIZE :, :] = jnp.concatenate(levels, axis=0).astype(jnp.bfloat16)


def attend(
    groups, lengths, base, queries, query_first, own, prompts, first_head, group_width, flops=1
):
    requests = queries.shape[0]
    heads = prompts.shape[2] // (2 * HEAD_SIZE)
    pieces, piece = prompts.shape[0], prompts.shape[3]
    query_rows = group_width * HEAD_SIZE
    width = group_width * FRESH_TOKENS
    place = lambda r, h, *_: (r, first_head + h, 0)
    by_head = lambda r, h, *_: (r, h, 0)
    specs = [
        pl.BlockSpec((1, query_rows, FRESH_TOKENS), lambda r, h, *_: (r, query_first + h, 0))
    ]
    if own:
        specs += [
            pl.BlockSpec((1, HEAD_SIZE, FRESH_TOKENS), place),
            pl.BlockSpec((1, HEAD_SIZE, FRESH_TOKENS), place),
            pl.BlockSpec((1, HEAD_SIZE, WINDOW_SPAN), place),
            pl.BlockSpec((1, HEAD_SIZE, WINDOW_SPAN), place),
        ]
    specs.append(
        pl.BlockSpec(
            (pieces, 1, 2 * HEAD_SIZE, piece), lambda r, h, group, *_: (0, group[r], h, 0)
        )
    )
    return pl.pallas_call(
        functools.partial(attention_kernel, bool(own)),
        grid_spec=pltpu.PrefetchScalarGridSpec(
            num_scalar_prefetch=3,
            grid=(requests, heads),
            in_specs=specs,
            out_specs=pl.BlockSpec((1, query_rows + LEVEL_ROWS, FRESH_TOKENS), by_head),
            scratch_shapes=[
                pltpu.VMEM((HEAD_SIZE, width), jnp.bfloat16),
                pltpu.VMEM((HEAD_SIZE + SUM_ROWS, width), jnp.float32),
                pltpu.VMEM((CACHE_BLOCK, width), jnp.float32),
                pltpu.VMEM((CACHE_BLOCK, width), jnp.float32),
            ],
        ),
        out_shape=jax.ShapeDtypeStruct(
            (requests, heads * (query_rows + LEVEL_ROWS), FRESH_TOKENS), jnp.bfloat16
        ),
        compiler_params=pltpu.CompilerParams(
            dimension_semantics=("arbitrary", "arbitrary"), vmem_limit_bytes=60 * 1024 * 1024
        ),
        cost_estimate=pl.CostEstimate(flops=flops, bytes_accessed=1, transcendentals=0),
        name="attend",
    )(groups, lengths, base, queries, *own, prompts)


def merge(parts, heads, group_width):
    requests = parts[0].shape[0]
    query_rows = group_width * HEAD_SIZE
    outs, levels = [], []
    for part in parts:
        rows = part.reshape(requests, heads, query_rows + LEVEL_ROWS, FRESH_TOKENS)
        rows = rows.astype(jnp.float32)
        outs.append(
            rows[:, :, :query_rows].reshape(requests, heads, group_width, HEAD_SIZE, FRESH_TOKENS)
        )
        terms = rows[:, :, query_rows : query_rows + group_width * LEVEL_TERMS]
        levels.append(
            terms.reshape(requests, heads, group_width, LEVEL_TERMS, FRESH_TOKENS).sum(
                axis=3, keepdims=True
            )
        )
    top = functools.reduce(jnp.maximum, levels)
    shares = [jnp.exp(level - top) for level in levels]
    summed = sum(out * share for out, share in zip(outs, shares, strict=True))
    merged = (summed / sum(shares)).astype(jnp.bfloat16)
    return merged.reshape(requests, heads * query_rows, FRESH_TOKENS)


def merge_kernel(sizes, group_width, rank_ref, *refs):
    *parts, mine_ref, sent_ref = refs
    low = rank_ref[0] == 0
    query_rows = group_width * HEAD_SIZE
    kept = mine_ref.shape[2]

    def level(ref, request, row):
        terms = ref[request, row : row + LEVEL_ROWS, :].astype(jnp.float32)
        return [
            sum(terms[LEVEL_TERMS * g + t : LEVEL_TERMS * g + t + 1] for t in range(LEVEL_TERMS))
            for g in range(group_width)
        ]

    start = 0
    for index, heads in enumerate(sizes):
        near_ref, far_ref = parts[2 * index : 2 * index + 2]
        for request in range(near_ref.shape[0]):
            for head in range(heads):
                row = head * (query_rows + LEVEL_ROWS)
                near_levels = level(near_ref, request, row + query_rows)
                far_levels = level(far_ref, request, row + query_rows)
                for g in range(group_width):
                    top = jnp.maximum(near_levels[g], far_levels[g])
                    near_share = jnp.exp(near_levels[g] - top)
                    far_share = jnp.exp(far_levels[g] - top)
                    whole = 1.0 / (near_share + far_share)
                    rows = slice(row + g * HEAD_SIZE, row + (g + 1) * HEAD_SIZE)
                    merged = near_ref[request, rows, :].astype(jnp.float32) * (
                        near_share * whole
                    ) + far_ref[request, rows, :].astype(jnp.float32) * (far_share * whole)
                    merged = merged.astype(jnp.bfloat16)
                    first, second = merged[:, :kept], merged[:, kept:]
                    place = start + head * query_rows + g * HEAD_SIZE
                    place = slice(place, place + HEAD_SIZE)
                    mine_ref[request, place, :] = jnp.where(low, first, second)
                    sent_ref[request, place, :] = jnp.where(low, second, first)
        start += heads * query_rows


def merge_split(rank, parts, sizes, group_width):
    half = jax.ShapeDtypeStruct(
        (parts[0].shape[0], sum(sizes) * group_width * HEAD_SIZE, FRESH_TOKENS // 2), jnp.bfloat16
    )
    vmem = pl.BlockSpec(memory_space=pltpu.VMEM)
    return pl.pallas_call(
        functools.partial(merge_kernel, sizes, group_width),
        in_specs=[pl.BlockSpec(memory_space=pltpu.SMEM)] + [vmem] * len(parts),
        out_specs=[vmem, vmem],
        out_shape=[half, half],
        compiler_params=pltpu.CompilerParams(vmem_limit_bytes=32 * 1024 * 1024),
        name="merge",
    )(rank, *parts)


def finish_kernel(own_count, got_count, plan, place_ref, *refs):
    tokens_ref, gain_ref, out_weight_ref, *refs = refs
    own, refs = refs[:own_count], refs[own_count:]
    got, refs = refs[:got_count], refs[got_count:]
    if got:
        out_mine_ref, out_core_ref, *refs = refs
    weights = refs[:-7]
    out_ref, normed_ref, total_ref, gate_ref, up_ref, down_ref, arrived = refs[-7:]
    step = pl.program_id(0)
    requests, rows = tokens_ref.shape[:2]
    tile = gate_ref.shape[2]
    slots = gate_ref.shape[0]

    def copies(index):
        gate, gate_block, up, up_block, down, down_block = plan[index]
        slot = index % slots
        if gate_block == "side":
            gate_block = place_ref[0]
        elif gate_block == "far":
            gate_block = 1 - place_ref[0]
        gate_columns = pl.ds(pl.multiple_of(gate_block * tile, tile), tile)
        up_columns = pl.ds(up_block * tile, tile)
        down_rows = pl.ds(down_block * tile, tile)
        return [
            pltpu.make_async_copy(
                weights[gate].at[:, gate_columns], gate_ref.at[slot], arrived.at[slot, 0]
            ),
            pltpu.make_async_copy(
                weights[up].at[:, up_columns], up_ref.at[slot], arrived.at[slot, 1]
            ),
            pltpu.make_async_copy(
                weights[down].at[down_rows, :], down_ref.at[slot], arrived.at[slot, 2]
            ),
        ]

    @pl.when(step == 0)
    def _():
        for index in range(min(slots - 1, len(plan))):
            for copy in copies(index):
                copy.start()
        for request in range(requests):
            summed = tokens_ref[request].astype(jnp.float32) + jnp.dot(
                jnp.concatenate([ref[request] for ref in own], axis=0).T,
                out_weight_ref[...],
                preferred_element_type=jnp.float32,
            )
            if got:
                heads = jnp.concatenate([ref[request] for ref in got], axis=0)
                half = heads.shape[0] // 2
                first_core = place_ref[1] == 0
                for ref, swapped in ((out_mine_ref, False), (out_core_ref, True)):
                    met = jnp.where(first_core != swapped, heads[:half], heads[half:])
                    summed = summed + jnp.dot(
                        met.T, ref[...], preferred_element_type=jnp.float32
                    )
            place = slice(request * rows, (request + 1) * rows)
            residual = summed.astype(jnp.bfloat16)
            normed_ref[place, :] = norm_rows(residual, gain_ref[...])
            total_ref[place, :] = residual.astype(jnp.float32)

    for index in range(len(plan)):

        @pl.when(step == index)
        def _(index=index):
            if index + slots - 1 < len(plan):
                for copy in copies(index + slots - 1):
                    copy.start()
            for copy in copies(index):
                copy.wait()

    slot = step % slots
    normed = normed_ref[...]
    gate = jnp.dot(normed, gate_ref[slot], preferred_element_type=jnp.float32)
    up = jnp.dot(normed, up_ref[slot], preferred_element_type=jnp.float32)
    hidden = (gate / (1.0 + jnp.exp(-gate)) * up).astype(jnp.bfloat16)
    total_ref[...] += jnp.dot(hidden, down_ref[slot], preferred_element_type=jnp.float32)

    @pl.when(step == len(plan) - 1)
    def _():
        for request in range(requests):
            out_ref[request] = total_ref[request * rows : (request + 1) * rows, :].astype(
                jnp.bfloat16
            )


def finish(place, tokens, gain, out_weight, own, got, out_fetched, weights, plan, tile):
    requests, rows, width = tokens.shape
    operands = [tokens, gain.reshape(1, width), out_weight, *own, *got, *out_fetched]
    specs = [
        pl.BlockSpec(
            array.shape,
            lambda *_, dims=array.ndim: (0,) * dims,
            pipeline_mode=pl.Buffered(1),
        )
        for array in operands
    ]
    operands += weights
    specs += [pl.BlockSpec(memory_space=pl.ANY)] * len(weights)
    slots = 3
    return pl.pallas_call(
        functools.partial(finish_kernel, len(own), len(got), plan),
        grid_spec=pltpu.PrefetchScalarGridSpec(
            num_scalar_prefetch=1,
            grid=(len(plan),),
            in_specs=specs,
            out_specs=pl.BlockSpec((requests, rows, width), lambda *_: (0, 0, 0)),
            scratch_shapes=[
                pltpu.VMEM((requests * rows, width), jnp.bfloat16),
                pltpu.VMEM((requests * rows, width), jnp.float32),
                pltpu.VMEM((slots, width, tile), jnp.bfloat16),
                pltpu.VMEM((slots, width, tile), jnp.bfloat16),
                pltpu.VMEM((slots, tile, width), jnp.bfloat16),
                pltpu.SemaphoreType.DMA((slots, 3)),
            ],
        ),
        out_shape=jax.ShapeDtypeStruct((requests, rows, width), jnp.bfloat16),
        compiler_params=pltpu.CompilerParams(
            dimension_semantics=("arbitrary",), vmem_limit_bytes=56 * 1024 * 1024
        ),
        name="finish",
    )(place, *operands)


def body(
    dp_size,
    tensor_size,
    tokens,
    cached_len,
    prompt_group,
    attn_gain,
    w_query,
    key_matrix,
    value_matrix,
    w_out,
    window_cache_keys,
    window_cache_values,
    prompt_keys,
    prompt_values,
    mlp_gain,
    w_gate,
    w_up,
    w_down,
):
    local_rows, local_reqs = tokens.shape[:2]
    query_cols = w_query.shape[1]
    key_cols = key_matrix.shape[1]
    key_heads = key_cols // HEAD_SIZE
    hidden_cols = w_gate.shape[1]
    paired = tensor_size == 2 and dp_size % 4 == 0 and key_heads == 4
    swap = [(0, 1), (1, 0)]
    half_dp = dp_size // 2
    halves = [list(range(half_dp)), list(range(half_dp, dp_size))]
    to_core = [(rank, rank ^ 1) for rank in range(dp_size)]
    to_side = [(rank, rank ^ 2) for rank in range(dp_size)]
    to_half = [(rank, (rank + half_dp) % dp_size) for rank in range(dp_size)]
    tensor_rank = lax.axis_index("tensor")
    rank = lax.axis_index("dp")
    core, side = rank % 2, rank // 2 % 2

    own_tokens = tokens.transpose(1, 0, 2)
    source = norm_rows(own_tokens, attn_gain)

    sizes = [2, 1, 1] if key_heads == 4 else [key_heads]
    starts = [sum(sizes[:chunk]) for chunk in range(len(sizes))]
    chunks = len(sizes)
    group_count, piece = prompt_keys.shape[:2]
    by_head = lambda a: a.transpose(0, 2, 1).reshape(group_count, key_heads, HEAD_SIZE, piece)
    packed = jnp.concatenate([by_head(prompt_keys), by_head(prompt_values)], axis=2)
    parts = [
        packed[:, start : start + size].reshape(group_count, size * 2 * HEAD_SIZE, piece)
        for start, size in zip(starts, sizes, strict=True)
    ]
    gather = lambda part: lax.all_gather(part, "dp", axis=0, axis_index_groups=halves)
    prompts = [gather(parts[0])]
    base = (rank // half_dp * (half_dp * piece)).reshape(1)
    about = jnp.concatenate([cached_len, prompt_group])
    about_far = lax.ppermute(about, "dp", to_half)

    past = [window_cache_keys.transpose(0, 2, 1), window_cache_values.transpose(0, 2, 1)]
    sent = []
    if paired:
        other = lax.ppermute(source, "tensor", swap)
        for weight, axis, share in ((w_out, 0, 2), (w_up, 1, 4), (w_down, 0, 4), (w_gate, 1, 2)):
            count = weight.shape[axis] // 4
            start = core * 2 * count + (side * count if share == 4 else 0)
            sent.append(lax.dynamic_slice_in_dim(weight, start, weight.shape[axis] // share, axis))
        other, sent, past = lax.optimization_barrier((other, sent, past))
        out_mine = lax.ppermute(sent[0], "tensor", swap)
        low = tensor_rank == 0
        normed = jnp.concatenate(
            [jnp.where(low, source, other), jnp.where(low, other, source)], axis=1
        )
    else:
        normed = lax.all_gather(source, "tensor", axis=1, tiled=True)

    positions = (
        PROMPT_TOKENS + cached_len[:, None] + jnp.arange(FRESH_TOKENS, dtype=jnp.int32)[None, :]
    )

    def project(weight):
        return jnp.stack(
            [
                lax.dot_general(
                    weight,
                    normed[request],
                    (((0,), (1,)), ((), ())),
                    preferred_element_type=jnp.float32,
                )
                for request in range(local_reqs)
            ]
        )

    queries = rotate_columns(project(w_query), positions)
    group_width = query_cols // key_cols
    head_rows = group_width * HEAD_SIZE
    cut = sizes[0] * head_rows
    asked, asked_rest = queries[:, :cut], queries[:, cut:]
    asked_far = lax.ppermute(asked, "dp", to_half)

    to_next = lambda part: lax.ppermute(part, "dp", to_side)
    hand = lambda part: lax.ppermute(part, "dp", to_core)

    held = (prompts[0], asked_rest, about_far)
    if paired:
        parts[1:], held, out_mine, sent[1:] = lax.optimization_barrier(
            (parts[1:], held, out_mine, sent[1:])
        )
        up_mine, down_mine = [lax.ppermute(part, "tensor", swap) for part in sent[1:3]]
        out_core = hand(out_mine)
    else:
        parts[1:], held = lax.optimization_barrier((parts[1:], held))
    prompts[0], asked_rest, about_far = held
    prompts += [gather(part) for part in parts[1:]]

    own = [
        rotate_columns(project(key_matrix), positions),
        project(value_matrix).astype(jnp.bfloat16),
    ]
    asked_far, asked_rest, own, prompts[0] = lax.optimization_barrier(
        (asked_far, asked_rest, own, prompts[0])
    )
    own += past
    asked_far = [asked_far]
    if chunks > 1:
        asked_far.append(lax.ppermute(asked_rest, "dp", to_half))
    if paired:
        asked_far[0], up_mine = lax.optimization_barrier((asked_far[0], up_mine))
        up_side, up_core = to_next(up_mine), hand(up_mine)

    far_lens, far_groups = about_far[:local_reqs], about_far[local_reqs:]
    far, near = [None] * chunks, [None] * chunks

    def attend_far(chunk):
        far[chunk] = attend(
            far_groups,
            far_lens,
            base,
            asked_far[min(chunk, 1)],
            max(chunk - 1, 0),
            [],
            prompts[chunk],
            0,
            group_width,
        )

    def attend_near(chunk):
        near[chunk] = attend(
            prompt_group,
            cached_len,
            base,
            queries,
            starts[chunk],
            own,
            prompts[chunk],
            starts[chunk],
            group_width,
            LAST_FLOPS if chunk == chunks - 1 else 1,
        )

    def send_back(chunk):
        far[chunk] = lax.ppermute(far[chunk], "dp", to_half)

    if paired:
        tile = hidden_cols // 4
        rank_ref = tensor_rank.reshape(1)
        attend_far(0)
        far[0], asked_far[1], down_mine, gate_sent, out_core = lax.optimization_barrier(
            (far[0], asked_far[1], down_mine, sent[3], out_core)
        )
        send_back(0)
        gate_mine = lax.ppermute(gate_sent, "tensor", swap)
        down_side, down_core = to_next(down_mine), hand(down_mine)
        attend_far(1)
        far[1], queries = lax.optimization_barrier((far[1], queries))
        send_back(1)
        attend_near(0)
        near[0], queries = lax.optimization_barrier((near[0], queries))
        attend_near(1)
        near[1], asked_far[1], up_core = lax.optimization_barrier((near[1], asked_far[1], up_core))
        attend_far(2)
        far[2], queries, far[:2], down_core = lax.optimization_barrier(
            (far[2], queries, far[:2], down_core)
        )
        send_back(2)
        queries, gate_mine, up_side = lax.optimization_barrier((queries, gate_mine, up_side))
        gate_core, up_far = hand(gate_mine), hand(up_side)
        kept_first, sent_first = merge_split(
            rank_ref, [near[0], far[0], near[1], far[1]], sizes[:2], group_width
        )
        swapped_first = lax.ppermute(sent_first, "tensor", swap)
        attend_near(2)
        near[2], far[2], swapped_first = lax.optimization_barrier(
            (near[2], far[2], swapped_first)
        )
        kept_last, sent_last = merge_split(rank_ref, [near[2], far[2]], sizes[2:], group_width)
        sent_last, down_side = lax.optimization_barrier((sent_last, down_side))
        swapped_last = lax.ppermute(sent_last, "tensor", swap)
        kept, swapped = [kept_first, kept_last], [swapped_first, swapped_last]
        weights = [w_gate, w_up, w_down, gate_mine, up_mine, down_mine, up_side, down_side]
        weights += [gate_core, up_core, down_core, up_far, hand(down_side)]
        plan = [(0, block, 1, block, 2, block) for block in range(4)]
        plan += [(3, "side", 4, 0, 5, 0), (3, "far", 6, 0, 7, 0)]
        plan += [(8, "side", 9, 0, 10, 0), (8, "far", 11, 0, 12, 0)]
        out_weight, got, out_fetched = w_out, swapped, [out_mine, out_core]
    else:
        kept, got, out_fetched = [], [], []
        for chunk in range(chunks):
            attend_far(chunk)
            send_back(chunk)
            attend_near(chunk)
            attended = merge([near[chunk], far[chunk]], sizes[chunk], group_width)
            kept.append(attended)
        attended = jnp.concatenate(kept, axis=1)
        kept = [lax.all_to_all(attended, "tensor", split_axis=2, concat_axis=1, tiled=True)]
        out_weight, *weights = [
            lax.all_gather(weight, "tensor", axis=axis, tiled=True)
            for weight, axis in ((w_out, 0), (w_gate, 1), (w_up, 1), (w_down, 0))
        ]
        tile = min(HIDDEN_TILE, hidden_cols)
        plan = [(0, block, 1, block, 2, block) for block in range(weights[0].shape[1] // tile)]
    place = jnp.stack([side, core])
    result = finish(
        place, own_tokens, mlp_gain, out_weight, kept, got, out_fetched, weights, plan, tile
    )
    return result.transpose(1, 0, 2)


def solution(mesh):
    in_specs = (
        P("tensor", "dp", None),
        P("dp"),
        P("dp"),
        P(),
        P(None, "tensor"),
        P(None, "tensor"),
        P(None, "tensor"),
        P("tensor", None),
        P("dp", None, "tensor"),
        P("dp", None, "tensor"),
        P(None, "dp", "tensor"),
        P(None, "dp", "tensor"),
        P(),
        P(None, "tensor"),
        P(None, "tensor"),
        P("tensor", None),
    )
    out_specs = P("tensor", "dp", None)
    return jax.shard_map(
        functools.partial(body, mesh.shape["dp"], mesh.shape["tensor"]),
        mesh=mesh,
        in_specs=in_specs,
        out_specs=out_specs,
        check_vma=False,
    )
```

```python
import functools
import math

import jax
import jax.numpy as jnp
from jax import lax
from jax.experimental import pallas as pl
from jax.experimental.pallas import tpu as pltpu
from jax.sharding import PartitionSpec as P

MODEL_WIDTH = 1536
HEAD_SIZE = 96
FRESH_TOKENS = 512
WINDOW_SPAN = 4096
SINKS = 4
PROMPT_TOKENS = 4096

rope_base = 10000.0
epsilon = 1e-05
far_below = -1e30
EXP2_SCALE = math.log2(math.e) / math.sqrt(HEAD_SIZE)
QUERY_TILE = 256
CACHE_BLOCK = 256
SUM_ROWS = 16
SCORE_SCALE = 1.0 / math.sqrt(HEAD_SIZE)
HIDDEN_TILE = 512
LEVEL_TERMS = 3
LEVEL_ROWS = 16
LAST_FLOPS = 15 * 10**9


def norm_rows(values, gain_vec):
    widened = values.astype(jnp.float32)
    factor = lax.rsqrt(jnp.mean(widened * widened, axis=-1, keepdims=True) + epsilon)
    return (widened * factor * gain_vec).astype(jnp.bfloat16)


def rotate_columns(values, positions):
    requests, rows, tokens = values.shape
    half_dim = HEAD_SIZE // 2
    frequency = rope_base ** (-2.0 * jnp.arange(half_dim, dtype=jnp.float32) / HEAD_SIZE)
    angles = positions.astype(jnp.float32)[:, None, None, :] * frequency[None, None, :, None]
    cosine = jnp.cos(angles)
    sine_part = jnp.sin(angles)
    split = values.reshape(requests, rows // HEAD_SIZE, 2, half_dim, tokens)
    first_half = split[:, :, 0]
    second_half = split[:, :, 1]
    turned = jnp.concatenate(
        [
            first_half * cosine - second_half * sine_part,
            second_half * cosine + first_half * sine_part,
        ],
        axis=2,
    )
    return turned.astype(jnp.bfloat16).reshape(requests, rows, tokens)


def attention_kernel(own, group_ref, len_ref, base_ref, q_ref, *refs):
    if own:
        fresh_k_ref, fresh_v_ref, cache_k_ref, cache_v_ref, *refs = refs
    prompt_ref, out_ref, wide_ref, sum_ref, even_ref, odd_ref = refs
    base = base_ref[0]
    length = len_ref[pl.program_id(0)]
    heads = q_ref.shape[1] // HEAD_SIZE
    pieces, piece = prompt_ref.shape[0], prompt_ref.shape[3]
    width = heads * FRESH_TOKENS
    tiles = [slice(start, start + QUERY_TILE) for start in range(0, width, QUERY_TILE)]
    for head in range(heads):
        wide_ref[:, head * FRESH_TOKENS : (head + 1) * FRESH_TOKENS] = q_ref[
            0, head * HEAD_SIZE : (head + 1) * HEAD_SIZE, :
        ]
    sum_ref[...] = jnp.zeros(sum_ref.shape, jnp.float32)

    def load_fresh(index):
        columns = slice(index * QUERY_TILE, (index + 1) * QUERY_TILE)
        return fresh_k_ref[0, :, columns], fresh_v_ref[0, :, columns]

    def load_cache(index):
        columns = pl.ds(pl.multiple_of(index * CACHE_BLOCK, CACHE_BLOCK), CACHE_BLOCK)
        return cache_k_ref[0, :, columns], cache_v_ref[0, :, columns]

    def load_prompt(index):
        return (
            prompt_ref[index, 0, 0:HEAD_SIZE, :],
            prompt_ref[index, 0, HEAD_SIZE : 2 * HEAD_SIZE, :],
        )

    def widen(values):
        return jnp.concatenate(
            [values, jnp.ones((SUM_ROWS, values.shape[1]), jnp.bfloat16)], axis=0
        )

    def digest(widened, scores, old_peak, tile):
        new_peak = jnp.maximum(old_peak, jnp.max(scores, axis=0, keepdims=True))
        weights = jnp.exp2((scores - new_peak) * EXP2_SCALE).astype(jnp.bfloat16)
        factor = jnp.exp2((old_peak - new_peak) * EXP2_SCALE)
        sum_ref[:, tile] = sum_ref[:, tile] * factor + jnp.dot(
            widened, weights, preferred_element_type=jnp.float32
        )
        return new_peak

    def masked_step(peak, loaded, visible, least=0):
        keys, values = loaded
        turned = keys.T
        widened = widen(values)
        scores = []
        for tile in tiles:
            raw = jnp.dot(turned, wide_ref[:, tile], preferred_element_type=jnp.float32)
            key_ids = lax.broadcasted_iota(jnp.int32, raw.shape, 0)
            row_ids = lax.broadcasted_iota(jnp.int32, raw.shape, 1) + tile.start % FRESH_TOKENS
            scores.append(jnp.where(visible(key_ids, row_ids), raw, far_below))
        peaks = []
        for tile, score in zip(tiles, scores, strict=True):
            old = peak[:, tile]
            if tile.start % FRESH_TOKENS + QUERY_TILE <= least:
                peaks.append(old)
            else:
                peaks.append(digest(widened, score, old, tile))
        return jnp.concatenate(peaks, axis=1)

    def score_into(loaded, held_ref):
        turned = loaded[0].T
        for tile in tiles:
            held_ref[0 : turned.shape[0], tile] = jnp.dot(
                turned, wide_ref[:, tile], preferred_element_type=jnp.float32
            )

    def digest_all(loaded, peak, held_ref, visible):
        widened = widen(loaded[1])
        block = widened.shape[1]
        peaks = []
        for tile in tiles:
            score = held_ref[0:block, tile]
            if visible is not None:
                key_ids = lax.broadcasted_iota(jnp.int32, score.shape, 0)
                row_ids = lax.broadcasted_iota(jnp.int32, score.shape, 1)
                row_ids = row_ids + tile.start % FRESH_TOKENS
                score = jnp.where(visible(key_ids, row_ids), score, far_below)
            peaks.append(digest(widened, score, peak[:, tile], tile))
        return jnp.concatenate(peaks, axis=1)

    def stream(low, high, load, peak, visible=lambda index: None):
        last = high - 1
        count = jnp.maximum(high - low, 0)

        def pair(step, peak):
            at = low + 2 * step
            score_into(load(at + 1), odd_ref)
            peak = digest_all(load(at), peak, even_ref, visible(at))
            score_into(load(jnp.minimum(at + 2, last)), even_ref)
            return digest_all(load(at + 1), peak, odd_ref, visible(at + 1))

        @pl.when(count > 0)
        def _():
            score_into(load(low), even_ref)

        peak = lax.fori_loop(0, count // 2, pair, peak)
        return lax.fori_loop(
            0,
            count % 2,
            lambda _, peak: digest_all(load(last), peak, even_ref, visible(last)),
            peak,
        )

    def cache_visible(index):
        start = index * CACHE_BLOCK
        return lambda keys, rows: (keys + start >= WINDOW_SPAN - length) & (keys + start > rows)

    def prompt_visible(index):
        start = base + index * piece
        return lambda keys, rows: (keys + start < SINKS) | (keys + start > length + rows)

    peak = jnp.full((1, width), far_below, jnp.float32)
    if own:
        for index in range(FRESH_TOKENS // QUERY_TILE):
            start = index * QUERY_TILE
            peak = masked_step(
                peak,
                load_fresh(index),
                lambda keys, rows, start=start: keys + start <= rows,
                least=start,
            )
        cache_blocks = WINDOW_SPAN // CACHE_BLOCK
        first = jnp.maximum((WINDOW_SPAN - length) // CACHE_BLOCK, 0)
        clear = jnp.minimum(jnp.maximum(first + 1, FRESH_TOKENS // CACHE_BLOCK), cache_blocks)
        peak = stream(first, clear, load_cache, peak, cache_visible)
        peak = stream(clear, cache_blocks, load_cache, peak)

    begin = jnp.clip((length + 1 - base) // piece, 0, pieces)
    open_from = jnp.clip((length + FRESH_TOKENS - 1 - base) // piece + 1, begin, pieces)
    sinks = jnp.where((base == 0) & (begin > 0), 1, 0)
    peak = lax.fori_loop(
        0,
        sinks,
        lambda index, peak: masked_step(peak, load_prompt(index), prompt_visible(index)),
        peak,
    )
    peak = stream(begin, open_from, load_prompt, peak, prompt_visible)
    peak = stream(open_from, pieces, load_prompt, peak)

    levels = []
    for head in range(heads):
        columns = slice(head * FRESH_TOKENS, (head + 1) * FRESH_TOKENS)
        total = sum_ref[:, columns]
        row_total = jnp.maximum(total[HEAD_SIZE : HEAD_SIZE + 1], 1e-30)
        out_ref[0, head * HEAD_SIZE : (head + 1) * HEAD_SIZE, :] = (
            total[:HEAD_SIZE] / row_total
        ).astype(jnp.bfloat16)
        rest = peak[:, columns] * SCORE_SCALE + jnp.log(row_total)
        for _ in range(LEVEL_TERMS):
            levels.append(rest.astype(jnp.bfloat16).astype(jnp.float32))
            rest = rest - levels[-1]
    levels.append(jnp.zeros((LEVEL_ROWS - len(levels), FRESH_TOKENS), jnp.float32))
    out_ref[0, heads * HEAD_SIZE :, :] = jnp.concatenate(levels, axis=0).astype(jnp.bfloat16)


def attend(
    groups, lengths, base, queries, query_first, own, prompts, first_head, group_width, flops=1
):
    requests = queries.shape[0]
    heads = prompts.shape[2] // (2 * HEAD_SIZE)
    pieces, piece = prompts.shape[0], prompts.shape[3]
    query_rows = group_width * HEAD_SIZE
    width = group_width * FRESH_TOKENS
    place = lambda r, h, *_: (r, first_head + h, 0)
    by_head = lambda r, h, *_: (r, h, 0)
    specs = [
        pl.BlockSpec((1, query_rows, FRESH_TOKENS), lambda r, h, *_: (r, query_first + h, 0))
    ]
    if own:
        specs += [
            pl.BlockSpec((1, HEAD_SIZE, FRESH_TOKENS), place),
            pl.BlockSpec((1, HEAD_SIZE, FRESH_TOKENS), place),
            pl.BlockSpec((1, HEAD_SIZE, WINDOW_SPAN), place),
            pl.BlockSpec((1, HEAD_SIZE, WINDOW_SPAN), place),
        ]
    specs.append(
        pl.BlockSpec(
            (pieces, 1, 2 * HEAD_SIZE, piece), lambda r, h, group, *_: (0, group[r], h, 0)
        )
    )
    return pl.pallas_call(
        functools.partial(attention_kernel, bool(own)),
        grid_spec=pltpu.PrefetchScalarGridSpec(
            num_scalar_prefetch=3,
            grid=(requests, heads),
            in_specs=specs,
            out_specs=pl.BlockSpec((1, query_rows + LEVEL_ROWS, FRESH_TOKENS), by_head),
            scratch_shapes=[
                pltpu.VMEM((HEAD_SIZE, width), jnp.bfloat16),
                pltpu.VMEM((HEAD_SIZE + SUM_ROWS, width), jnp.float32),
                pltpu.VMEM((CACHE_BLOCK, width), jnp.float32),
                pltpu.VMEM((CACHE_BLOCK, width), jnp.float32),
            ],
        ),
        out_shape=jax.ShapeDtypeStruct(
            (requests, heads * (query_rows + LEVEL_ROWS), FRESH_TOKENS), jnp.bfloat16
        ),
        compiler_params=pltpu.CompilerParams(
            dimension_semantics=("arbitrary", "arbitrary"), vmem_limit_bytes=60 * 1024 * 1024
        ),
        cost_estimate=pl.CostEstimate(flops=flops, bytes_accessed=1, transcendentals=0),
        name="attend",
    )(groups, lengths, base, queries, *own, prompts)


def merge(parts, heads, group_width):
    requests = parts[0].shape[0]
    query_rows = group_width * HEAD_SIZE
    outs, levels = [], []
    for part in parts:
        rows = part.reshape(requests, heads, query_rows + LEVEL_ROWS, FRESH_TOKENS)
        rows = rows.astype(jnp.float32)
        outs.append(
            rows[:, :, :query_rows].reshape(requests, heads, group_width, HEAD_SIZE, FRESH_TOKENS)
        )
        terms = rows[:, :, query_rows : query_rows + group_width * LEVEL_TERMS]
        levels.append(
            terms.reshape(requests, heads, group_width, LEVEL_TERMS, FRESH_TOKENS).sum(
                axis=3, keepdims=True
            )
        )
    top = functools.reduce(jnp.maximum, levels)
    shares = [jnp.exp(level - top) for level in levels]
    summed = sum(out * share for out, share in zip(outs, shares, strict=True))
    merged = (summed / sum(shares)).astype(jnp.bfloat16)
    return merged.reshape(requests, heads * query_rows, FRESH_TOKENS)


def merge_kernel(sizes, group_width, rank_ref, *refs):
    *parts, mine_ref, sent_ref = refs
    low = rank_ref[0] == 0
    query_rows = group_width * HEAD_SIZE
    kept = mine_ref.shape[2]

    def level(ref, request, row):
        terms = ref[request, row : row + LEVEL_ROWS, :].astype(jnp.float32)
        return [
            sum(terms[LEVEL_TERMS * g + t : LEVEL_TERMS * g + t + 1] for t in range(LEVEL_TERMS))
            for g in range(group_width)
        ]

    start = 0
    for index, heads in enumerate(sizes):
        near_ref, far_ref = parts[2 * index : 2 * index + 2]
        for request in range(near_ref.shape[0]):
            for head in range(heads):
                row = head * (query_rows + LEVEL_ROWS)
                near_levels = level(near_ref, request, row + query_rows)
                far_levels = level(far_ref, request, row + query_rows)
                for g in range(group_width):
                    top = jnp.maximum(near_levels[g], far_levels[g])
                    near_share = jnp.exp(near_levels[g] - top)
                    far_share = jnp.exp(far_levels[g] - top)
                    whole = 1.0 / (near_share + far_share)
                    rows = slice(row + g * HEAD_SIZE, row + (g + 1) * HEAD_SIZE)
                    merged = near_ref[request, rows, :].astype(jnp.float32) * (
                        near_share * whole
                    ) + far_ref[request, rows, :].astype(jnp.float32) * (far_share * whole)
                    merged = merged.astype(jnp.bfloat16)
                    first, second = merged[:, :kept], merged[:, kept:]
                    place = start + head * query_rows + g * HEAD_SIZE
                    place = slice(place, place + HEAD_SIZE)
                    mine_ref[request, place, :] = jnp.where(low, first, second)
                    sent_ref[request, place, :] = jnp.where(low, second, first)
        start += heads * query_rows


def merge_split(rank, parts, sizes, group_width):
    half = jax.ShapeDtypeStruct(
        (parts[0].shape[0], sum(sizes) * group_width * HEAD_SIZE, FRESH_TOKENS // 2), jnp.bfloat16
    )
    vmem = pl.BlockSpec(memory_space=pltpu.VMEM)
    return pl.pallas_call(
        functools.partial(merge_kernel, sizes, group_width),
        in_specs=[pl.BlockSpec(memory_space=pltpu.SMEM)] + [vmem] * len(parts),
        out_specs=[vmem, vmem],
        out_shape=[half, half],
        compiler_params=pltpu.CompilerParams(vmem_limit_bytes=32 * 1024 * 1024),
        name="merge",
    )(rank, *parts)


def finish_kernel(own_count, got_count, plan, place_ref, *refs):
    tokens_ref, gain_ref, out_weight_ref, *refs = refs
    own, refs = refs[:own_count], refs[own_count:]
    got, refs = refs[:got_count], refs[got_count:]
    if got:
        out_mine_ref, out_core_ref, *refs = refs
    weights = refs[:-7]
    out_ref, normed_ref, total_ref, gate_ref, up_ref, down_ref, arrived = refs[-7:]
    step = pl.program_id(0)
    requests, rows = tokens_ref.shape[:2]
    tile = gate_ref.shape[2]
    slots = gate_ref.shape[0]

    def copies(index):
        gate, gate_block, up, up_block, down, down_block = plan[index]
        slot = index % slots
        if gate_block == "side":
            gate_block = place_ref[0]
        elif gate_block == "far":
            gate_block = 1 - place_ref[0]
        gate_columns = pl.ds(pl.multiple_of(gate_block * tile, tile), tile)
        up_columns = pl.ds(up_block * tile, tile)
        down_rows = pl.ds(down_block * tile, tile)
        return [
            pltpu.make_async_copy(
                weights[gate].at[:, gate_columns], gate_ref.at[slot], arrived.at[slot, 0]
            ),
            pltpu.make_async_copy(
                weights[up].at[:, up_columns], up_ref.at[slot], arrived.at[slot, 1]
            ),
            pltpu.make_async_copy(
                weights[down].at[down_rows, :], down_ref.at[slot], arrived.at[slot, 2]
            ),
        ]

    @pl.when(step == 0)
    def _():
        for index in range(min(slots - 1, len(plan))):
            for copy in copies(index):
                copy.start()
        for request in range(requests):
            summed = tokens_ref[request].astype(jnp.float32) + jnp.dot(
                jnp.concatenate([ref[request] for ref in own], axis=0).T,
                out_weight_ref[...],
                preferred_element_type=jnp.float32,
            )
            if got:
                heads = jnp.concatenate([ref[request] for ref in got], axis=0)
                half = heads.shape[0] // 2
                first_core = place_ref[1] == 0
                for ref, swapped in ((out_mine_ref, False), (out_core_ref, True)):
                    met = jnp.where(first_core != swapped, heads[:half], heads[half:])
                    summed = summed + jnp.dot(
                        met.T, ref[...], preferred_element_type=jnp.float32
                    )
            place = slice(request * rows, (request + 1) * rows)
            residual = summed.astype(jnp.bfloat16)
            normed_ref[place, :] = norm_rows(residual, gain_ref[...])
            total_ref[place, :] = residual.astype(jnp.float32)

    for index in range(len(plan)):

        @pl.when(step == index)
        def _(index=index):
            if index + slots - 1 < len(plan):
                for copy in copies(index + slots - 1):
                    copy.start()
            for copy in copies(index):
                copy.wait()

    slot = step % slots
    normed = normed_ref[...]
    gate = jnp.dot(normed, gate_ref[slot], preferred_element_type=jnp.float32)
    up = jnp.dot(normed, up_ref[slot], preferred_element_type=jnp.float32)
    hidden = (gate / (1.0 + jnp.exp(-gate)) * up).astype(jnp.bfloat16)
    total_ref[...] += jnp.dot(hidden, down_ref[slot], preferred_element_type=jnp.float32)

    @pl.when(step == len(plan) - 1)
    def _():
        for request in range(requests):
            out_ref[request] = total_ref[request * rows : (request + 1) * rows, :].astype(
                jnp.bfloat16
            )


def finish(place, tokens, gain, out_weight, own, got, out_fetched, weights, plan, tile):
    requests, rows, width = tokens.shape
    operands = [tokens, gain.reshape(1, width), out_weight, *own, *got, *out_fetched]
    specs = [
        pl.BlockSpec(
            array.shape,
            lambda *_, dims=array.ndim: (0,) * dims,
            pipeline_mode=pl.Buffered(1),
        )
        for array in operands
    ]
    operands += weights
    specs += [pl.BlockSpec(memory_space=pl.ANY)] * len(weights)
    slots = 3
    return pl.pallas_call(
        functools.partial(finish_kernel, len(own), len(got), plan),
        grid_spec=pltpu.PrefetchScalarGridSpec(
            num_scalar_prefetch=1,
            grid=(len(plan),),
            in_specs=specs,
            out_specs=pl.BlockSpec((requests, rows, width), lambda *_: (0, 0, 0)),
            scratch_shapes=[
                pltpu.VMEM((requests * rows, width), jnp.bfloat16),
                pltpu.VMEM((requests * rows, width), jnp.float32),
                pltpu.VMEM((slots, width, tile), jnp.bfloat16),
                pltpu.VMEM((slots, width, tile), jnp.bfloat16),
                pltpu.VMEM((slots, tile, width), jnp.bfloat16),
                pltpu.SemaphoreType.DMA((slots, 3)),
            ],
        ),
        out_shape=jax.ShapeDtypeStruct((requests, rows, width), jnp.bfloat16),
        compiler_params=pltpu.CompilerParams(
            dimension_semantics=("arbitrary",), vmem_limit_bytes=56 * 1024 * 1024
        ),
        name="finish",
    )(place, *operands)


def body(
    dp_size,
    tensor_size,
    tokens,
    cached_len,
    prompt_group,
    attn_gain,
    w_query,
    key_matrix,
    value_matrix,
    w_out,
    window_cache_keys,
    window_cache_values,
    prompt_keys,
    prompt_values,
    mlp_gain,
    w_gate,
    w_up,
    w_down,
):
    local_rows, local_reqs = tokens.shape[:2]
    query_cols = w_query.shape[1]
    key_cols = key_matrix.shape[1]
    key_heads = key_cols // HEAD_SIZE
    hidden_cols = w_gate.shape[1]
    paired = tensor_size == 2 and dp_size % 4 == 0 and key_heads == 4
    swap = [(0, 1), (1, 0)]
    half_dp = dp_size // 2
    halves = [list(range(half_dp)), list(range(half_dp, dp_size))]
    to_core = [(rank, rank ^ 1) for rank in range(dp_size)]
    to_side = [(rank, rank ^ 2) for rank in range(dp_size)]
    to_half = [(rank, (rank + half_dp) % dp_size) for rank in range(dp_size)]
    tensor_rank = lax.axis_index("tensor")
    rank = lax.axis_index("dp")
    core, side = rank % 2, rank // 2 % 2

    own_tokens = tokens.transpose(1, 0, 2)
    source = norm_rows(own_tokens, attn_gain)

    sizes = [2, 1, 1] if key_heads == 4 else [key_heads]
    starts = [sum(sizes[:chunk]) for chunk in range(len(sizes))]
    chunks = len(sizes)
    group_count, piece = prompt_keys.shape[:2]
    by_head = lambda a: a.transpose(0, 2, 1).reshape(group_count, key_heads, HEAD_SIZE, piece)
    packed = jnp.concatenate([by_head(prompt_keys), by_head(prompt_values)], axis=2)
    parts = [
        packed[:, start : start + size].reshape(group_count, size * 2 * HEAD_SIZE, piece)
        for start, size in zip(starts, sizes, strict=True)
    ]
    gather = lambda part: lax.all_gather(part, "dp", axis=0, axis_index_groups=halves)
    prompts = [gather(parts[0])]
    base = (rank // half_dp * (half_dp * piece)).reshape(1)
    about = jnp.concatenate([cached_len, prompt_group])
    about_far = lax.ppermute(about, "dp", to_half)

    past = [window_cache_keys.transpose(0, 2, 1), window_cache_values.transpose(0, 2, 1)]
    sent = []
    if paired:
        other = lax.ppermute(source, "tensor", swap)
        for weight, axis, share in ((w_out, 0, 2), (w_up, 1, 4), (w_down, 0, 4), (w_gate, 1, 2)):
            count = weight.shape[axis] // 4
            start = core * 2 * count + (side * count if share == 4 else 0)
            sent.append(lax.dynamic_slice_in_dim(weight, start, weight.shape[axis] // share, axis))
        other, sent, past = lax.optimization_barrier((other, sent, past))
        out_mine = lax.ppermute(sent[0], "tensor", swap)
        low = tensor_rank == 0
        normed = jnp.concatenate(
            [jnp.where(low, source, other), jnp.where(low, other, source)], axis=1
        )
    else:
        normed = lax.all_gather(source, "tensor", axis=1, tiled=True)

    positions = (
        PROMPT_TOKENS + cached_len[:, None] + jnp.arange(FRESH_TOKENS, dtype=jnp.int32)[None, :]
    )

    def project(weight):
        return jnp.stack(
            [
                lax.dot_general(
                    weight,
                    normed[request],
                    (((0,), (1,)), ((), ())),
                    preferred_element_type=jnp.float32,
                )
                for request in range(local_reqs)
            ]
        )

    queries = rotate_columns(project(w_query), positions)
    group_width = query_cols // key_cols
    head_rows = group_width * HEAD_SIZE
    cut = sizes[0] * head_rows
    asked, asked_rest = queries[:, :cut], queries[:, cut:]
    asked_far = lax.ppermute(asked, "dp", to_half)

    to_next = lambda part: lax.ppermute(part, "dp", to_side)
    hand = lambda part: lax.ppermute(part, "dp", to_core)

    held = (prompts[0], asked_rest, about_far)
    if paired:
        parts[1:], held, out_mine, sent[1:] = lax.optimization_barrier(
            (parts[1:], held, out_mine, sent[1:])
        )
        up_mine, down_mine = [lax.ppermute(part, "tensor", swap) for part in sent[1:3]]
        out_core = hand(out_mine)
    else:
        parts[1:], held = lax.optimization_barrier((parts[1:], held))
    prompts[0], asked_rest, about_far = held
    prompts += [gather(part) for part in parts[1:]]

    own = [
        rotate_columns(project(key_matrix), positions),
        project(value_matrix).astype(jnp.bfloat16),
    ]
    asked_far, asked_rest, own, prompts[0] = lax.optimization_barrier(
        (asked_far, asked_rest, own, prompts[0])
    )
    own += past
    asked_far = [asked_far]
    if chunks > 1:
        asked_far.append(lax.ppermute(asked_rest, "dp", to_half))
    if paired:
        asked_far[0], up_mine = lax.optimization_barrier((asked_far[0], up_mine))
        up_side, up_core = to_next(up_mine), hand(up_mine)

    far_lens, far_groups = about_far[:local_reqs], about_far[local_reqs:]
    far, near = [None] * chunks, [None] * chunks

    def attend_far(chunk):
        far[chunk] = attend(
            far_groups,
            far_lens,
            base,
            asked_far[min(chunk, 1)],
            max(chunk - 1, 0),
            [],
            prompts[chunk],
            0,
            group_width,
        )

    def attend_near(chunk):
        near[chunk] = attend(
            prompt_group,
            cached_len,
            base,
            queries,
            starts[chunk],
            own,
            prompts[chunk],
            starts[chunk],
            group_width,
            LAST_FLOPS if chunk == chunks - 1 else 1,
        )

    def send_back(chunk):
        far[chunk] = lax.ppermute(far[chunk], "dp", to_half)

    if paired:
        tile = hidden_cols // 4
        rank_ref = tensor_rank.reshape(1)
        attend_far(0)
        far[0], asked_far[1], down_mine, gate_sent, out_core = lax.optimization_barrier(
            (far[0], asked_far[1], down_mine, sent[3], out_core)
        )
        send_back(0)
        gate_mine = lax.ppermute(gate_sent, "tensor", swap)
        down_side, down_core = to_next(down_mine), hand(down_mine)
        attend_far(1)
        far[1], queries = lax.optimization_barrier((far[1], queries))
        send_back(1)
        attend_near(0)
        near[0], queries = lax.optimization_barrier((near[0], queries))
        attend_near(1)
        near[1], asked_far[1], up_core = lax.optimization_barrier((near[1], asked_far[1], up_core))
        attend_far(2)
        far[2], queries, far[:2], down_core = lax.optimization_barrier(
            (far[2], queries, far[:2], down_core)
        )
        send_back(2)
        queries, gate_mine, up_side = lax.optimization_barrier((queries, gate_mine, up_side))
        gate_core, up_far = hand(gate_mine), hand(up_side)
        kept_first, sent_first = merge_split(
            rank_ref, [near[0], far[0], near[1], far[1]], sizes[:2], group_width
        )
        swapped_first = lax.ppermute(sent_first, "tensor", swap)
        attend_near(2)
        near[2], far[2], swapped_first = lax.optimization_barrier(
            (near[2], far[2], swapped_first)
        )
        kept_last, sent_last = merge_split(rank_ref, [near[2], far[2]], sizes[2:], group_width)
        swapped_last = lax.ppermute(sent_last, "tensor", swap)
        swapped_last, down_side = lax.optimization_barrier((swapped_last, down_side))
        kept, swapped = [kept_first, kept_last], [swapped_first, swapped_last]
        weights = [w_gate, w_up, w_down, gate_mine, up_mine, down_mine, up_side, down_side]
        weights += [gate_core, up_core, down_core, up_far, hand(down_side)]
        plan = [(0, block, 1, block, 2, block) for block in range(4)]
        plan += [(3, "side", 4, 0, 5, 0), (3, "far", 6, 0, 7, 0)]
        plan += [(8, "side", 9, 0, 10, 0), (8, "far", 11, 0, 12, 0)]
        out_weight, got, out_fetched = w_out, swapped, [out_mine, out_core]
    else:
        kept, got, out_fetched = [], [], []
        for chunk in range(chunks):
            attend_far(chunk)
            send_back(chunk)
            attend_near(chunk)
            attended = merge([near[chunk], far[chunk]], sizes[chunk], group_width)
            kept.append(attended)
        attended = jnp.concatenate(kept, axis=1)
        kept = [lax.all_to_all(attended, "tensor", split_axis=2, concat_axis=1, tiled=True)]
        out_weight, *weights = [
            lax.all_gather(weight, "tensor", axis=axis, tiled=True)
            for weight, axis in ((w_out, 0), (w_gate, 1), (w_up, 1), (w_down, 0))
        ]
        tile = min(HIDDEN_TILE, hidden_cols)
        plan = [(0, block, 1, block, 2, block) for block in range(weights[0].shape[1] // tile)]
    place = jnp.stack([side, core])
    result = finish(
        place, own_tokens, mlp_gain, out_weight, kept, got, out_fetched, weights, plan, tile
    )
    return result.transpose(1, 0, 2)


def solution(mesh):
    in_specs = (
        P("tensor", "dp", None),
        P("dp"),
        P("dp"),
        P(),
        P(None, "tensor"),
        P(None, "tensor"),
        P(None, "tensor"),
        P("tensor", None),
        P("dp", None, "tensor"),
        P("dp", None, "tensor"),
        P(None, "dp", "tensor"),
        P(None, "dp", "tensor"),
        P(),
        P(None, "tensor"),
        P(None, "tensor"),
        P("tensor", None),
    )
    out_specs = P("tensor", "dp", None)
    return jax.shard_map(
        functools.partial(body, mesh.shape["dp"], mesh.shape["tensor"]),
        mesh=mesh,
        in_specs=in_specs,
        out_specs=out_specs,
        check_vma=False,
    )
```

```python
import functools
import math

import jax
import jax.numpy as jnp
from jax import lax
from jax.experimental import pallas as pl
from jax.experimental.pallas import tpu as pltpu
from jax.sharding import PartitionSpec as P

MODEL_WIDTH = 1536
HEAD_SIZE = 96
FRESH_TOKENS = 512
WINDOW_SPAN = 4096
SINKS = 4
PROMPT_TOKENS = 4096

rope_base = 10000.0
epsilon = 1e-05
far_below = -1e30
EXP2_SCALE = math.log2(math.e) / math.sqrt(HEAD_SIZE)
QUERY_TILE = 256
CACHE_BLOCK = 256
SUM_ROWS = 16
SCORE_SCALE = 1.0 / math.sqrt(HEAD_SIZE)
HIDDEN_TILE = 512
LEVEL_TERMS = 3
LEVEL_ROWS = 16
LAST_FLOPS = 15 * 10**9


def norm_rows(values, gain_vec):
    widened = values.astype(jnp.float32)
    factor = lax.rsqrt(jnp.mean(widened * widened, axis=-1, keepdims=True) + epsilon)
    return (widened * factor * gain_vec).astype(jnp.bfloat16)


def rotate_columns(values, positions):
    requests, rows, tokens = values.shape
    half_dim = HEAD_SIZE // 2
    frequency = rope_base ** (-2.0 * jnp.arange(half_dim, dtype=jnp.float32) / HEAD_SIZE)
    angles = positions.astype(jnp.float32)[:, None, None, :] * frequency[None, None, :, None]
    cosine = jnp.cos(angles)
    sine_part = jnp.sin(angles)
    split = values.reshape(requests, rows // HEAD_SIZE, 2, half_dim, tokens)
    first_half = split[:, :, 0]
    second_half = split[:, :, 1]
    turned = jnp.concatenate(
        [
            first_half * cosine - second_half * sine_part,
            second_half * cosine + first_half * sine_part,
        ],
        axis=2,
    )
    return turned.astype(jnp.bfloat16).reshape(requests, rows, tokens)


def attention_kernel(own, group_ref, len_ref, base_ref, q_ref, *refs):
    if own:
        fresh_k_ref, fresh_v_ref, cache_k_ref, cache_v_ref, *refs = refs
    prompt_ref, out_ref, wide_ref, sum_ref, even_ref, odd_ref = refs
    base = base_ref[0]
    length = len_ref[pl.program_id(0)]
    heads = q_ref.shape[1] // HEAD_SIZE
    pieces, piece = prompt_ref.shape[0], prompt_ref.shape[3]
    width = heads * FRESH_TOKENS
    tiles = [slice(start, start + QUERY_TILE) for start in range(0, width, QUERY_TILE)]
    for head in range(heads):
        wide_ref[:, head * FRESH_TOKENS : (head + 1) * FRESH_TOKENS] = q_ref[
            0, head * HEAD_SIZE : (head + 1) * HEAD_SIZE, :
        ]
    sum_ref[...] = jnp.zeros(sum_ref.shape, jnp.float32)

    def load_fresh(index):
        columns = slice(index * QUERY_TILE, (index + 1) * QUERY_TILE)
        return fresh_k_ref[0, :, columns], fresh_v_ref[0, :, columns]

    def load_cache(index):
        columns = pl.ds(pl.multiple_of(index * CACHE_BLOCK, CACHE_BLOCK), CACHE_BLOCK)
        return cache_k_ref[0, :, columns], cache_v_ref[0, :, columns]

    def load_prompt(index):
        return (
            prompt_ref[index, 0, 0:HEAD_SIZE, :],
            prompt_ref[index, 0, HEAD_SIZE : 2 * HEAD_SIZE, :],
        )

    def widen(values):
        return jnp.concatenate(
            [values, jnp.ones((SUM_ROWS, values.shape[1]), jnp.bfloat16)], axis=0
        )

    def digest(widened, scores, old_peak, tile):
        new_peak = jnp.maximum(old_peak, jnp.max(scores, axis=0, keepdims=True))
        weights = jnp.exp2((scores - new_peak) * EXP2_SCALE).astype(jnp.bfloat16)
        factor = jnp.exp2((old_peak - new_peak) * EXP2_SCALE)
        sum_ref[:, tile] = sum_ref[:, tile] * factor + jnp.dot(
            widened, weights, preferred_element_type=jnp.float32
        )
        return new_peak

    def masked_step(peak, loaded, visible, least=0):
        keys, values = loaded
        turned = keys.T
        widened = widen(values)
        scores = []
        for tile in tiles:
            raw = jnp.dot(turned, wide_ref[:, tile], preferred_element_type=jnp.float32)
            key_ids = lax.broadcasted_iota(jnp.int32, raw.shape, 0)
            row_ids = lax.broadcasted_iota(jnp.int32, raw.shape, 1) + tile.start % FRESH_TOKENS
            scores.append(jnp.where(visible(key_ids, row_ids), raw, far_below))
        peaks = []
        for tile, score in zip(tiles, scores, strict=True):
            old = peak[:, tile]
            if tile.start % FRESH_TOKENS + QUERY_TILE <= least:
                peaks.append(old)
            else:
                peaks.append(digest(widened, score, old, tile))
        return jnp.concatenate(peaks, axis=1)

    def score_into(loaded, held_ref):
        turned = loaded[0].T
        for tile in tiles:
            held_ref[0 : turned.shape[0], tile] = jnp.dot(
                turned, wide_ref[:, tile], preferred_element_type=jnp.float32
            )

    def digest_all(loaded, peak, held_ref, visible):
        widened = widen(loaded[1])
        block = widened.shape[1]
        peaks = []
        for tile in tiles:
            score = held_ref[0:block, tile]
            if visible is not None:
                key_ids = lax.broadcasted_iota(jnp.int32, score.shape, 0)
                row_ids = lax.broadcasted_iota(jnp.int32, score.shape, 1)
                row_ids = row_ids + tile.start % FRESH_TOKENS
                score = jnp.where(visible(key_ids, row_ids), score, far_below)
            peaks.append(digest(widened, score, peak[:, tile], tile))
        return jnp.concatenate(peaks, axis=1)

    def stream(low, high, load, peak, visible=lambda index: None):
        last = high - 1
        count = jnp.maximum(high - low, 0)

        def pair(step, peak):
            at = low + 2 * step
            score_into(load(at + 1), odd_ref)
            peak = digest_all(load(at), peak, even_ref, visible(at))
            score_into(load(jnp.minimum(at + 2, last)), even_ref)
            return digest_all(load(at + 1), peak, odd_ref, visible(at + 1))

        @pl.when(count > 0)
        def _():
            score_into(load(low), even_ref)

        peak = lax.fori_loop(0, count // 2, pair, peak)
        return lax.fori_loop(
            0,
            count % 2,
            lambda _, peak: digest_all(load(last), peak, even_ref, visible(last)),
            peak,
        )

    def cache_visible(index):
        start = index * CACHE_BLOCK
        return lambda keys, rows: (keys + start >= WINDOW_SPAN - length) & (keys + start > rows)

    def prompt_visible(index):
        start = base + index * piece
        return lambda keys, rows: (keys + start < SINKS) | (keys + start > length + rows)

    peak = jnp.full((1, width), far_below, jnp.float32)
    if own:
        for index in range(FRESH_TOKENS // QUERY_TILE):
            start = index * QUERY_TILE
            peak = masked_step(
                peak,
                load_fresh(index),
                lambda keys, rows, start=start: keys + start <= rows,
                least=start,
            )
        cache_blocks = WINDOW_SPAN // CACHE_BLOCK
        first = jnp.maximum((WINDOW_SPAN - length) // CACHE_BLOCK, 0)
        clear = jnp.minimum(jnp.maximum(first + 1, FRESH_TOKENS // CACHE_BLOCK), cache_blocks)
        peak = stream(first, clear, load_cache, peak, cache_visible)
        peak = stream(clear, cache_blocks, load_cache, peak)

    begin = jnp.clip((length + 1 - base) // piece, 0, pieces)
    open_from = jnp.clip((length + FRESH_TOKENS - 1 - base) // piece + 1, begin, pieces)
    sinks = jnp.where((base == 0) & (begin > 0), 1, 0)
    peak = lax.fori_loop(
        0,
        sinks,
        lambda index, peak: masked_step(peak, load_prompt(index), prompt_visible(index)),
        peak,
    )
    peak = stream(begin, open_from, load_prompt, peak, prompt_visible)
    peak = stream(open_from, pieces, load_prompt, peak)

    levels = []
    for head in range(heads):
        columns = slice(head * FRESH_TOKENS, (head + 1) * FRESH_TOKENS)
        total = sum_ref[:, columns]
        row_total = jnp.maximum(total[HEAD_SIZE : HEAD_SIZE + 1], 1e-30)
        out_ref[0, head * HEAD_SIZE : (head + 1) * HEAD_SIZE, :] = (
            total[:HEAD_SIZE] / row_total
        ).astype(jnp.bfloat16)
        rest = peak[:, columns] * SCORE_SCALE + jnp.log(row_total)
        for _ in range(LEVEL_TERMS):
            levels.append(rest.astype(jnp.bfloat16).astype(jnp.float32))
            rest = rest - levels[-1]
    levels.append(jnp.zeros((LEVEL_ROWS - len(levels), FRESH_TOKENS), jnp.float32))
    out_ref[0, heads * HEAD_SIZE :, :] = jnp.concatenate(levels, axis=0).astype(jnp.bfloat16)


def attend(
    groups, lengths, base, queries, query_first, own, prompts, first_head, group_width, flops=1
):
    requests = queries.shape[0]
    heads = prompts.shape[2] // (2 * HEAD_SIZE)
    pieces, piece = prompts.shape[0], prompts.shape[3]
    query_rows = group_width * HEAD_SIZE
    width = group_width * FRESH_TOKENS
    place = lambda r, h, *_: (r, first_head + h, 0)
    by_head = lambda r, h, *_: (r, h, 0)
    specs = [
        pl.BlockSpec((1, query_rows, FRESH_TOKENS), lambda r, h, *_: (r, query_first + h, 0))
    ]
    if own:
        specs += [
            pl.BlockSpec((1, HEAD_SIZE, FRESH_TOKENS), place),
            pl.BlockSpec((1, HEAD_SIZE, FRESH_TOKENS), place),
            pl.BlockSpec((1, HEAD_SIZE, WINDOW_SPAN), place),
            pl.BlockSpec((1, HEAD_SIZE, WINDOW_SPAN), place),
        ]
    specs.append(
        pl.BlockSpec(
            (pieces, 1, 2 * HEAD_SIZE, piece), lambda r, h, group, *_: (0, group[r], h, 0)
        )
    )
    return pl.pallas_call(
        functools.partial(attention_kernel, bool(own)),
        grid_spec=pltpu.PrefetchScalarGridSpec(
            num_scalar_prefetch=3,
            grid=(requests, heads),
            in_specs=specs,
            out_specs=pl.BlockSpec((1, query_rows + LEVEL_ROWS, FRESH_TOKENS), by_head),
            scratch_shapes=[
                pltpu.VMEM((HEAD_SIZE, width), jnp.bfloat16),
                pltpu.VMEM((HEAD_SIZE + SUM_ROWS, width), jnp.float32),
                pltpu.VMEM((CACHE_BLOCK, width), jnp.float32),
                pltpu.VMEM((CACHE_BLOCK, width), jnp.float32),
            ],
        ),
        out_shape=jax.ShapeDtypeStruct(
            (requests, heads * (query_rows + LEVEL_ROWS), FRESH_TOKENS), jnp.bfloat16
        ),
        compiler_params=pltpu.CompilerParams(
            dimension_semantics=("arbitrary", "arbitrary"), vmem_limit_bytes=60 * 1024 * 1024
        ),
        cost_estimate=pl.CostEstimate(flops=flops, bytes_accessed=1, transcendentals=0),
        name="attend",
    )(groups, lengths, base, queries, *own, prompts)


def merge(parts, heads, group_width):
    requests = parts[0].shape[0]
    query_rows = group_width * HEAD_SIZE
    outs, levels = [], []
    for part in parts:
        rows = part.reshape(requests, heads, query_rows + LEVEL_ROWS, FRESH_TOKENS)
        rows = rows.astype(jnp.float32)
        outs.append(
            rows[:, :, :query_rows].reshape(requests, heads, group_width, HEAD_SIZE, FRESH_TOKENS)
        )
        terms = rows[:, :, query_rows : query_rows + group_width * LEVEL_TERMS]
        levels.append(
            terms.reshape(requests, heads, group_width, LEVEL_TERMS, FRESH_TOKENS).sum(
                axis=3, keepdims=True
            )
        )
    top = functools.reduce(jnp.maximum, levels)
    shares = [jnp.exp(level - top) for level in levels]
    summed = sum(out * share for out, share in zip(outs, shares, strict=True))
    merged = (summed / sum(shares)).astype(jnp.bfloat16)
    return merged.reshape(requests, heads * query_rows, FRESH_TOKENS)


def merge_kernel(sizes, group_width, rank_ref, *refs):
    *parts, mine_ref, sent_ref = refs
    low = rank_ref[0] == 0
    query_rows = group_width * HEAD_SIZE
    kept = mine_ref.shape[2]

    def level(ref, request, row):
        terms = ref[request, row : row + LEVEL_ROWS, :].astype(jnp.float32)
        return [
            sum(terms[LEVEL_TERMS * g + t : LEVEL_TERMS * g + t + 1] for t in range(LEVEL_TERMS))
            for g in range(group_width)
        ]

    start = 0
    for index, heads in enumerate(sizes):
        near_ref, far_ref = parts[2 * index : 2 * index + 2]
        for request in range(near_ref.shape[0]):
            for head in range(heads):
                row = head * (query_rows + LEVEL_ROWS)
                near_levels = level(near_ref, request, row + query_rows)
                far_levels = level(far_ref, request, row + query_rows)
                for g in range(group_width):
                    top = jnp.maximum(near_levels[g], far_levels[g])
                    near_share = jnp.exp(near_levels[g] - top)
                    far_share = jnp.exp(far_levels[g] - top)
                    whole = 1.0 / (near_share + far_share)
                    rows = slice(row + g * HEAD_SIZE, row + (g + 1) * HEAD_SIZE)
                    merged = near_ref[request, rows, :].astype(jnp.float32) * (
                        near_share * whole
                    ) + far_ref[request, rows, :].astype(jnp.float32) * (far_share * whole)
                    merged = merged.astype(jnp.bfloat16)
                    first, second = merged[:, :kept], merged[:, kept:]
                    place = start + head * query_rows + g * HEAD_SIZE
                    place = slice(place, place + HEAD_SIZE)
                    mine_ref[request, place, :] = jnp.where(low, first, second)
                    sent_ref[request, place, :] = jnp.where(low, second, first)
        start += heads * query_rows


def merge_split(rank, parts, sizes, group_width):
    half = jax.ShapeDtypeStruct(
        (parts[0].shape[0], sum(sizes) * group_width * HEAD_SIZE, FRESH_TOKENS // 2), jnp.bfloat16
    )
    vmem = pl.BlockSpec(memory_space=pltpu.VMEM)
    return pl.pallas_call(
        functools.partial(merge_kernel, sizes, group_width),
        in_specs=[pl.BlockSpec(memory_space=pltpu.SMEM)] + [vmem] * len(parts),
        out_specs=[vmem, vmem],
        out_shape=[half, half],
        compiler_params=pltpu.CompilerParams(vmem_limit_bytes=32 * 1024 * 1024),
        name="merge",
    )(rank, *parts)


def finish_kernel(own_count, got_count, plan, place_ref, *refs):
    tokens_ref, gain_ref, out_weight_ref, *refs = refs
    own, refs = refs[:own_count], refs[own_count:]
    got, refs = refs[:got_count], refs[got_count:]
    if got:
        out_mine_ref, out_core_ref, *refs = refs
    weights = refs[:-7]
    out_ref, normed_ref, total_ref, gate_ref, up_ref, down_ref, arrived = refs[-7:]
    step = pl.program_id(0)
    requests, rows = tokens_ref.shape[:2]
    tile = gate_ref.shape[2]
    slots = gate_ref.shape[0]

    def copies(index):
        gate, gate_block, up, up_block, down, down_block = plan[index]
        slot = index % slots
        if gate_block == "side":
            gate_block = place_ref[0]
        elif gate_block == "far":
            gate_block = 1 - place_ref[0]
        gate_columns = pl.ds(pl.multiple_of(gate_block * tile, tile), tile)
        up_columns = pl.ds(up_block * tile, tile)
        down_rows = pl.ds(down_block * tile, tile)
        return [
            pltpu.make_async_copy(
                weights[gate].at[:, gate_columns], gate_ref.at[slot], arrived.at[slot, 0]
            ),
            pltpu.make_async_copy(
                weights[up].at[:, up_columns], up_ref.at[slot], arrived.at[slot, 1]
            ),
            pltpu.make_async_copy(
                weights[down].at[down_rows, :], down_ref.at[slot], arrived.at[slot, 2]
            ),
        ]

    @pl.when(step == 0)
    def _():
        for index in range(min(slots - 1, len(plan))):
            for copy in copies(index):
                copy.start()
        for request in range(requests):
            summed = tokens_ref[request].astype(jnp.float32) + jnp.dot(
                jnp.concatenate([ref[request] for ref in own], axis=0).T,
                out_weight_ref[...],
                preferred_element_type=jnp.float32,
            )
            if got:
                heads = jnp.concatenate([ref[request] for ref in got], axis=0)
                half = heads.shape[0] // 2
                first_core = place_ref[1] == 0
                for ref, swapped in ((out_mine_ref, False), (out_core_ref, True)):
                    met = jnp.where(first_core != swapped, heads[:half], heads[half:])
                    summed = summed + jnp.dot(
                        met.T, ref[...], preferred_element_type=jnp.float32
                    )
            place = slice(request * rows, (request + 1) * rows)
            residual = summed.astype(jnp.bfloat16)
            normed_ref[place, :] = norm_rows(residual, gain_ref[...])
            total_ref[place, :] = residual.astype(jnp.float32)

    for index in range(len(plan)):

        @pl.when(step == index)
        def _(index=index):
            if index + slots - 1 < len(plan):
                for copy in copies(index + slots - 1):
                    copy.start()
            for copy in copies(index):
                copy.wait()

    slot = step % slots
    normed = normed_ref[...]
    gate = jnp.dot(normed, gate_ref[slot], preferred_element_type=jnp.float32)
    up = jnp.dot(normed, up_ref[slot], preferred_element_type=jnp.float32)
    hidden = (gate / (1.0 + jnp.exp(-gate)) * up).astype(jnp.bfloat16)
    total_ref[...] += jnp.dot(hidden, down_ref[slot], preferred_element_type=jnp.float32)

    @pl.when(step == len(plan) - 1)
    def _():
        for request in range(requests):
            out_ref[request] = total_ref[request * rows : (request + 1) * rows, :].astype(
                jnp.bfloat16
            )


def finish(place, tokens, gain, out_weight, own, got, out_fetched, weights, plan, tile):
    requests, rows, width = tokens.shape
    operands = [tokens, gain.reshape(1, width), out_weight, *own, *got, *out_fetched]
    specs = [
        pl.BlockSpec(
            array.shape,
            lambda *_, dims=array.ndim: (0,) * dims,
            pipeline_mode=pl.Buffered(1),
        )
        for array in operands
    ]
    operands += weights
    specs += [pl.BlockSpec(memory_space=pl.ANY)] * len(weights)
    slots = 3
    return pl.pallas_call(
        functools.partial(finish_kernel, len(own), len(got), plan),
        grid_spec=pltpu.PrefetchScalarGridSpec(
            num_scalar_prefetch=1,
            grid=(len(plan),),
            in_specs=specs,
            out_specs=pl.BlockSpec((requests, rows, width), lambda *_: (0, 0, 0)),
            scratch_shapes=[
                pltpu.VMEM((requests * rows, width), jnp.bfloat16),
                pltpu.VMEM((requests * rows, width), jnp.float32),
                pltpu.VMEM((slots, width, tile), jnp.bfloat16),
                pltpu.VMEM((slots, width, tile), jnp.bfloat16),
                pltpu.VMEM((slots, tile, width), jnp.bfloat16),
                pltpu.SemaphoreType.DMA((slots, 3)),
            ],
        ),
        out_shape=jax.ShapeDtypeStruct((requests, rows, width), jnp.bfloat16),
        compiler_params=pltpu.CompilerParams(
            dimension_semantics=("arbitrary",), vmem_limit_bytes=56 * 1024 * 1024
        ),
        name="finish",
    )(place, *operands)


def body(
    dp_size,
    tensor_size,
    tokens,
    cached_len,
    prompt_group,
    attn_gain,
    w_query,
    key_matrix,
    value_matrix,
    w_out,
    window_cache_keys,
    window_cache_values,
    prompt_keys,
    prompt_values,
    mlp_gain,
    w_gate,
    w_up,
    w_down,
):
    local_rows, local_reqs = tokens.shape[:2]
    query_cols = w_query.shape[1]
    key_cols = key_matrix.shape[1]
    key_heads = key_cols // HEAD_SIZE
    hidden_cols = w_gate.shape[1]
    paired = tensor_size == 2 and dp_size % 4 == 0 and key_heads == 4
    swap = [(0, 1), (1, 0)]
    half_dp = dp_size // 2
    halves = [list(range(half_dp)), list(range(half_dp, dp_size))]
    to_core = [(rank, rank ^ 1) for rank in range(dp_size)]
    to_side = [(rank, rank ^ 2) for rank in range(dp_size)]
    to_half = [(rank, (rank + half_dp) % dp_size) for rank in range(dp_size)]
    tensor_rank = lax.axis_index("tensor")
    rank = lax.axis_index("dp")
    core, side = rank % 2, rank // 2 % 2

    own_tokens = tokens.transpose(1, 0, 2)
    source = norm_rows(own_tokens, attn_gain)

    sizes = [2, 1, 1] if key_heads == 4 else [key_heads]
    starts = [sum(sizes[:chunk]) for chunk in range(len(sizes))]
    chunks = len(sizes)
    group_count, piece = prompt_keys.shape[:2]
    by_head = lambda a: a.transpose(0, 2, 1).reshape(group_count, key_heads, HEAD_SIZE, piece)
    packed = jnp.concatenate([by_head(prompt_keys), by_head(prompt_values)], axis=2)
    parts = [
        packed[:, start : start + size].reshape(group_count, size * 2 * HEAD_SIZE, piece)
        for start, size in zip(starts, sizes, strict=True)
    ]
    gather = lambda part: lax.all_gather(part, "dp", axis=0, axis_index_groups=halves)
    prompts = [gather(parts[0])]
    base = (rank // half_dp * (half_dp * piece)).reshape(1)
    about = jnp.concatenate([cached_len, prompt_group])
    about_far = lax.ppermute(about, "dp", to_half)

    past = [window_cache_keys.transpose(0, 2, 1), window_cache_values.transpose(0, 2, 1)]
    sent = []
    if paired:
        other = lax.ppermute(source, "tensor", swap)
        for weight, axis, share in ((w_out, 0, 2), (w_up, 1, 4), (w_down, 0, 4), (w_gate, 1, 2)):
            count = weight.shape[axis] // 4
            start = core * 2 * count + (side * count if share == 4 else 0)
            sent.append(lax.dynamic_slice_in_dim(weight, start, weight.shape[axis] // share, axis))
        other, sent, past = lax.optimization_barrier((other, sent, past))
        out_mine = lax.ppermute(sent[0], "tensor", swap)
        low = tensor_rank == 0
        normed = jnp.concatenate(
            [jnp.where(low, source, other), jnp.where(low, other, source)], axis=1
        )
    else:
        normed = lax.all_gather(source, "tensor", axis=1, tiled=True)

    positions = (
        PROMPT_TOKENS + cached_len[:, None] + jnp.arange(FRESH_TOKENS, dtype=jnp.int32)[None, :]
    )

    def project(weight):
        return jnp.stack(
            [
                lax.dot_general(
                    weight,
                    normed[request],
                    (((0,), (1,)), ((), ())),
                    preferred_element_type=jnp.float32,
                )
                for request in range(local_reqs)
            ]
        )

    queries = rotate_columns(project(w_query), positions)
    group_width = query_cols // key_cols
    head_rows = group_width * HEAD_SIZE
    cut = sizes[0] * head_rows
    asked, asked_rest = queries[:, :cut], queries[:, cut:]
    asked_far = lax.ppermute(asked, "dp", to_half)

    to_next = lambda part: lax.ppermute(part, "dp", to_side)
    hand = lambda part: lax.ppermute(part, "dp", to_core)

    held = (prompts[0], asked_rest, about_far)
    if paired:
        parts[1:], held, out_mine, sent[1:] = lax.optimization_barrier(
            (parts[1:], held, out_mine, sent[1:])
        )
        up_mine, down_mine = [lax.ppermute(part, "tensor", swap) for part in sent[1:3]]
        out_core = hand(out_mine)
    else:
        parts[1:], held = lax.optimization_barrier((parts[1:], held))
    prompts[0], asked_rest, about_far = held
    prompts += [gather(part) for part in parts[1:]]

    own = [
        rotate_columns(project(key_matrix), positions),
        project(value_matrix).astype(jnp.bfloat16),
    ]
    asked_far, asked_rest, own, prompts[0] = lax.optimization_barrier(
        (asked_far, asked_rest, own, prompts[0])
    )
    own += past
    asked_far = [asked_far]
    if chunks > 1:
        asked_far.append(lax.ppermute(asked_rest, "dp", to_half))
    if paired:
        asked_far[0], up_mine = lax.optimization_barrier((asked_far[0], up_mine))
        up_side, up_core = to_next(up_mine), hand(up_mine)

    far_lens, far_groups = about_far[:local_reqs], about_far[local_reqs:]
    far, near = [None] * chunks, [None] * chunks

    def attend_far(chunk):
        far[chunk] = attend(
            far_groups,
            far_lens,
            base,
            asked_far[min(chunk, 1)],
            max(chunk - 1, 0),
            [],
            prompts[chunk],
            0,
            group_width,
        )

    def attend_near(chunk):
        near[chunk] = attend(
            prompt_group,
            cached_len,
            base,
            queries,
            starts[chunk],
            own,
            prompts[chunk],
            starts[chunk],
            group_width,
            LAST_FLOPS if chunk == chunks - 1 else 1,
        )

    def send_back(chunk):
        far[chunk] = lax.ppermute(far[chunk], "dp", to_half)

    if paired:
        tile = hidden_cols // 4
        rank_ref = tensor_rank.reshape(1)
        attend_far(0)
        far[0], asked_far[1], down_mine, gate_sent, out_core = lax.optimization_barrier(
            (far[0], asked_far[1], down_mine, sent[3], out_core)
        )
        send_back(0)
        gate_mine = lax.ppermute(gate_sent, "tensor", swap)
        down_side, down_core = to_next(down_mine), hand(down_mine)
        attend_far(1)
        far[1], queries = lax.optimization_barrier((far[1], queries))
        send_back(1)
        attend_near(0)
        near[0], queries = lax.optimization_barrier((near[0], queries))
        attend_near(1)
        near[1], asked_far[1], up_core = lax.optimization_barrier((near[1], asked_far[1], up_core))
        attend_far(2)
        far[2], queries, far[:2], down_core = lax.optimization_barrier(
            (far[2], queries, far[:2], down_core)
        )
        send_back(2)
        queries, gate_mine, up_side = lax.optimization_barrier((queries, gate_mine, up_side))
        gate_core, up_far = hand(gate_mine), hand(up_side)
        kept_first, sent_first = merge_split(
            rank_ref, [near[0], far[0], near[1], far[1]], sizes[:2], group_width
        )
        swapped_first = lax.ppermute(sent_first, "tensor", swap)
        attend_near(2)
        done_rows = kept_first.shape[1]
        own_tokens = own_tokens.astype(jnp.float32) + jnp.stack(
            [
                lax.dot_general(
                    kept_first[request],
                    w_out[:done_rows],
                    (((0,), (0,)), ((), ())),
                    preferred_element_type=jnp.float32,
                )
                for request in range(local_reqs)
            ]
        )
        near[2], far[2], swapped_first, own_tokens = lax.optimization_barrier(
            (near[2], far[2], swapped_first, own_tokens)
        )
        kept_last, sent_last = merge_split(rank_ref, [near[2], far[2]], sizes[2:], group_width)
        swapped_last = lax.ppermute(sent_last, "tensor", swap)
        swapped_last, down_side = lax.optimization_barrier((swapped_last, down_side))
        kept, swapped = [kept_last], [swapped_first, swapped_last]
        weights = [w_gate, w_up, w_down, gate_mine, up_mine, down_mine, up_side, down_side]
        weights += [gate_core, up_core, down_core, up_far, hand(down_side)]
        plan = [(0, block, 1, block, 2, block) for block in range(4)]
        plan += [(3, "side", 4, 0, 5, 0), (3, "far", 6, 0, 7, 0)]
        plan += [(8, "side", 9, 0, 10, 0), (8, "far", 11, 0, 12, 0)]
        out_weight, got, out_fetched = w_out[done_rows:], swapped, [out_mine, out_core]
    else:
        kept, got, out_fetched = [], [], []
        for chunk in range(chunks):
            attend_far(chunk)
            send_back(chunk)
            attend_near(chunk)
            attended = merge([near[chunk], far[chunk]], sizes[chunk], group_width)
            kept.append(attended)
        attended = jnp.concatenate(kept, axis=1)
        kept = [lax.all_to_all(attended, "tensor", split_axis=2, concat_axis=1, tiled=True)]
        out_weight, *weights = [
            lax.all_gather(weight, "tensor", axis=axis, tiled=True)
            for weight, axis in ((w_out, 0), (w_gate, 1), (w_up, 1), (w_down, 0))
        ]
        tile = min(HIDDEN_TILE, hidden_cols)
        plan = [(0, block, 1, block, 2, block) for block in range(weights[0].shape[1] // tile)]
    place = jnp.stack([side, core])
    result = finish(
        place, own_tokens, mlp_gain, out_weight, kept, got, out_fetched, weights, plan, tile
    )
    return result.transpose(1, 0, 2)


def solution(mesh):
    in_specs = (
        P("tensor", "dp", None),
        P("dp"),
        P("dp"),
        P(),
        P(None, "tensor"),
        P(None, "tensor"),
        P(None, "tensor"),
        P("tensor", None),
        P("dp", None, "tensor"),
        P("dp", None, "tensor"),
        P(None, "dp", "tensor"),
        P(None, "dp", "tensor"),
        P(),
        P(None, "tensor"),
        P(None, "tensor"),
        P("tensor", None),
    )
    out_specs = P("tensor", "dp", None)
    return jax.shard_map(
        functools.partial(body, mesh.shape["dp"], mesh.shape["tensor"]),
        mesh=mesh,
        in_specs=in_specs,
        out_specs=out_specs,
        check_vma=False,
    )
```
